32 devices in a mesh: user: 8 (over y, x, core), item: 4 (over z).
Axes of the slice: x: 2, y: 2, z: 4, core: 2. Of those that a mesh axis runs over, the one named last changes fastest.
Arguments:
- u_factors: float32 [65536, 256], P(('user', 'item')), may hold values from -1.5 to 1.5
- v_factors: float32 [16384, 256], P(('item', 'user')), may hold values from -1.5 to 1.5
- ratings: bfloat16 [8, 4, 2, 224, 128, 128], P('user', 'item'), may hold values from -6 to 6
- tile_rows: int32 [8, 4, 2, 224], P('user', 'item'), may hold values from 0 to 15, as said below
- tile_cols: int32 [8, 4, 2, 224], P('user', 'item'), may hold values from 0 to 31
- tile_counts: int32 [8, 4, 2], P('user', 'item'), may hold values from 28 to 224, as said below
- u_noise: bfloat16 [2, 65536, 256], P(None, ('user', 'item')), may hold values from -6 to 6
- v_noise: bfloat16 [2, 16384, 256], P(None, ('item', 'user')), may hold values from -6 to 6
Outputs:
- new_users: float32 [65536, 256], P(('user', 'item'))
- new_items: float32 [16384, 256], P(('item', 'user'))
The draws below stay inside these ranges and needn't reach their ends.
Inputs may be any that keep to these rules, and one draw needn't show every extreme that they name: Within one list of a block and sub-epoch the (tile_rows, tile_cols) pairs are distinct over all 224 slots. `tile_counts`: some list in every draw is full and some has the smallest count.
All inputs are finite; a program needn't handle non-finite values.
Results may differ from the reference program's by a relative error of at most 0.00115.
Values may be sent and summed in bfloat16 or wider, within the bound.
No kernel may reach another device: no remote copies, remote signals or barrier semaphores. Data moves between devices by JAX's collectives and lax.ppermute only.
A program may use at most 128 MiB of HBM per device.

```python
import math
import jax
import jax.numpy as jnp
from jax import lax

K = 256
TILE = 128
UT = 16
IT = 32
TPB = 224
SUBS = 2
USERS = 65536
ITEMS = 16384
N_USER = 8
N_ITEM = 4


def slot_lists(key):
    cells = N_USER * N_ITEM * SUBS
    subkeys = jax.random.split(jax.random.fold_in(key, 17), cells)
    slots = jax.vmap(lambda subkey: jax.random.permutation(subkey, UT * IT)[:TPB])(subkeys)
    return slots.reshape(N_USER, N_ITEM, SUBS, TPB).astype(jnp.int32)


def draw_tile_rows(key, part):
    return slot_lists(key) // IT


def draw_tile_cols(key, part):
    return slot_lists(key) % IT


def draw_tile_counts(key, part):
    cells = N_USER * N_ITEM * SUBS
    lowest = max(1, TPB // 8)
    spread = TPB - lowest
    keys = jax.random.split(jax.random.fold_in(key, 29), 4)
    first = jax.random.randint(keys[0], (cells,), 0, spread + 1)
    second = jax.random.randint(keys[1], (cells,), 0, spread + 1)
    counts = lowest + first * second // max(spread, 1)
    fullest = jax.random.randint(keys[2], (), 0, cells)
    emptiest = (fullest + 1 + jax.random.randint(keys[3], (), 0, cells - 1)) % cells
    places = jnp.arange(cells)
    counts = jnp.where(places == fullest, TPB, counts)
    counts = jnp.where(places == emptiest, lowest, counts)
    return counts.reshape(N_USER, N_ITEM, SUBS).astype(jnp.int32)


def block_levels(own_key, shape, cuts, smallest, high):
    level, own = 1.0, jax.random.fold_in(own_key, 6)
    for position, parts in cuts:
        heights = jnp.exp(jax.random.uniform(jax.random.fold_in(own, position), (parts,), jnp.float32, smallest / len(cuts), high / len(cuts)))
        level = level * jnp.repeat(heights, shape[position] // parts).reshape([-1 if axis == position else 1 for axis in range(len(shape))])
    return level


def scatter_about(rng, shape, scale, reach, shards=(), kind=jnp.bfloat16):
    values = scale * jax.random.normal(rng, shape, jnp.float32)
    if shards:
        values = values * block_levels(rng, shape, shards, -0.22, 0.18)
    return jnp.clip(values, -reach, reach).astype(kind)


def setup_inputs(seed: int = 0) -> dict:
    streams_of = jax.random.split(jax.random.key(seed), 9)
    return {
        "u_factors": scatter_about(streams_of[0], (USERS, K), 0.25, 1.5, ((0, 32),), jnp.float32),
        "v_factors": scatter_about(streams_of[1], (ITEMS, K), 0.25, 1.5, ((0, 32),), jnp.float32),
        "ratings": scatter_about(streams_of[2], (N_USER, N_ITEM, SUBS, TPB, TILE, TILE), 1.0, 6.0, ((0, 8), (1, 4))),
        "tile_rows": draw_tile_rows(jax.random.fold_in(streams_of[8], 71), 0),
        "tile_cols": draw_tile_cols(jax.random.fold_in(streams_of[8], 71), 0),
        "tile_counts": draw_tile_counts(jax.random.fold_in(streams_of[8], 71), 0),
        "u_noise": scatter_about(streams_of[6], (SUBS, USERS, K), 1.0, 6.0, ((1, 32),)),
        "v_noise": scatter_about(streams_of[7], (SUBS, ITEMS, K), 1.0, 6.0, ((1, 32),)),
    }


STEP_SIZE = 0.004
PRIOR = 25.0

def reference(u_factors, v_factors, ratings, tile_rows, tile_cols, tile_counts, u_noise, v_noise):
    power = float(N_ITEM)
    half_step = 0.5 * STEP_SIZE
    root_step = math.sqrt(STEP_SIZE)
    user_rows = UT * TILE
    group_rows = IT * TILE
    users_now = u_factors
    items_now = v_factors
    for section in range(SUBS):
        users_bf = users_now.astype(jnp.bfloat16)
        items_bf = items_now.astype(jnp.bfloat16)

        def block_work(carry, block):
            urow = block // N_ITEM
            icol = block % N_ITEM
            group = (icol - section) % N_ITEM
            user_tiles = lax.dynamic_slice_in_dim(users_bf, (block * user_rows).astype(jnp.int32), user_rows, 0)
            user_tiles = user_tiles.reshape(UT, TILE, K).astype(jnp.float32)
            item_tiles = lax.dynamic_slice_in_dim(items_bf, (group * group_rows).astype(jnp.int32), group_rows, 0)
            item_tiles = item_tiles.reshape(IT, TILE, K).astype(jnp.float32)
            rating_list = ratings[urow, icol, section]
            row_list = tile_rows[urow, icol, section]
            col_list = tile_cols[urow, icol, section]
            live_count = tile_counts[urow, icol, section]
            user_part = user_tiles[row_list]
            item_part = item_tiles[col_list]
            predicted = jnp.einsum('tak,tbk->tab', user_part, item_part)
            live = jnp.arange(TPB) < live_count
            misfit = jnp.where(live[:, None, None], rating_list.astype(jnp.float32) - predicted, 0.0).astype(jnp.bfloat16)
            misfit = lax.optimization_barrier(misfit).astype(jnp.float32)
            grad_user = jnp.zeros((UT, TILE, K), jnp.float32).at[row_list].add(jnp.einsum('tab,tbk->tak', misfit, item_part))
            grad_group = jnp.zeros((IT, TILE, K), jnp.float32).at[col_list].add(jnp.einsum('tab,tak->tbk', misfit, user_part))
            carry = carry.at[group].add(grad_group)
            return (carry, grad_user.reshape(user_rows, K))
        grad_items, grad_users = lax.scan(block_work, jnp.zeros((N_ITEM, IT, TILE, K), jnp.float32), jnp.arange(N_USER * N_ITEM, dtype=jnp.int32))
        grad_users = grad_users.reshape(USERS, K)
        grad_items = grad_items.reshape(ITEMS, K)
        users_now = users_now + half_step * (power * grad_users - PRIOR * users_now) + root_step * u_noise[section].astype(jnp.float32)
        noise_items = jnp.roll(v_noise[section].astype(jnp.float32).reshape(N_ITEM, group_rows, K), -section, axis=0).reshape(ITEMS, K)
        items_now = items_now + half_step * (power * grad_items - PRIOR * items_now) + root_step * noise_items
    return (users_now, items_now)
```

```python
import functools
import math

import jax
import jax.numpy as jnp
from jax import lax
from jax.experimental import pallas as pl
from jax.experimental.pallas import tpu as pltpu
from jax.sharding import PartitionSpec as P

HALF_STEP = 0.002
ROOT_STEP = math.sqrt(0.004)
PRIOR = 25.0
GROUP = 4
DEPTH = 16
SCALE_ROWS = 16
VMEM_LIMIT = 40 * 2**20

ANY = pl.BlockSpec(memory_space=pl.ANY)
IN_VMEM = pl.BlockSpec(memory_space=pltpu.VMEM)
IN_SMEM = pl.BlockSpec(memory_space=pltpu.SMEM)


def shifted(x, axis, by):
    peers = lax.axis_size(axis)
    return lax.ppermute(x, axis, [(i, (i + by) % peers) for i in range(peers)])


def swapped(x, axis, mask):
    peers = lax.axis_size(axis)
    return lax.ppermute(x, axis, [(i, i ^ mask) for i in range(peers)])


def widths(slots, user_tiles, item_tiles):
    bits = tuple(max(1, (n - 1).bit_length()) for n in (slots, user_tiles, item_tiles))
    assert 2 * bits[0] + 2 * bits[1] + bits[2] + 2 <= 31
    return bits


def pair_plan(rows, cols, count, me, user_tiles, item_tiles, per, span):
    slots = rows.shape[0]
    slot_bits, row_bits, col_bits = widths(slots, user_tiles, item_tiles)
    place = ((cols // per) ^ me) * per + cols % per
    n = jnp.arange(slots, dtype=jnp.int32)
    live = n < count
    same = (place[:, None] == place[None, :]) & live[None, :]
    rank = jnp.sum(same & (rows[None, :] < rows[:, None]), axis=1, dtype=jnp.int32)
    opens = live & (rank % 2 == 0)
    run = place // span
    runs = item_tiles // span
    run_ids = jnp.arange(runs, dtype=jnp.int32)
    ahead = (place[None, :] < place[:, None]) & (run[None, :] == run[:, None]) & opens[None, :]
    within = jnp.sum(ahead, axis=1, dtype=jnp.int32)
    size = jnp.sum((run[None, :] == run_ids[:, None]) & opens[None, :], axis=1, dtype=jnp.int32)
    size = (size + GROUP - 1) // GROUP * GROUP
    edges = jnp.arange(runs + 1, dtype=jnp.int32)
    starts = jnp.sum(jnp.where(run_ids[None, :] < edges[:, None], size[None, :], 0), axis=1, dtype=jnp.int32)
    base = jnp.sum(jnp.where(run_ids[None, :] < run[:, None], size[None, :], 0), axis=1, dtype=jnp.int32)
    where = base + within + rank // 2
    col_at = 2 * slot_bits + 2 * row_bits
    one = 1 << (col_at + col_bits)
    first = n | (rows << (2 * slot_bits)) | (place << col_at)
    second = (n << slot_bits) | (rows << (2 * slot_bits + row_bits))
    word = jnp.where(live, jnp.where(rank % 2 == 0, first, second) + one, 0)
    words = jnp.arange((slots + item_tiles) // 2 + runs * GROUP, dtype=jnp.int32)[:, None]
    pairs = jnp.sum(jnp.where(where[None, :] == words, word[None, :], 0), axis=1, dtype=jnp.int32)
    unused = jnp.sum(words >= starts[None, 1:], axis=1, dtype=jnp.int32) * span
    unused = jnp.minimum(unused, item_tiles - 1) << col_at
    return jnp.where(pairs == 0, unused, pairs), starts


def grads_kernel(section, first_run, last_run, span, bits, pieces, pairs, starts, ratings, users, *refs):
    piece_in = refs[:pieces]
    grad_user_out = refs[pieces]
    grad_item_out = refs[pieces + 1 : 2 * pieces + 1]
    items, rated, misfits, grad_user, grad_item, rated_sem, piece_sem, out_sem = refs[2 * pieces + 1 :]
    slot_bits, row_bits, col_bits = bits
    per = items.shape[0] // pieces
    tile = users.shape[1]
    low, high = starts[first_run], starts[last_run]
    steps = lax.div(high - low, GROUP)

    def decode(p):
        word = pairs[p]
        fields = []
        for width in (slot_bits, slot_bits, row_bits, row_bits, col_bits):
            fields.append(word & ((1 << width) - 1))
            word = word >> width
        fields[4] -= first_run * span
        return (*fields, word)

    def loads(p):
        slot = lax.rem(p - low, DEPTH)
        return [
            pltpu.make_async_copy(
                ratings.at[section, n], rated.at[slot, pl.ds(half * tile, tile)], rated_sem.at[slot, half]
            )
            for half, n in enumerate(decode(p)[:2])
        ]

    def issue(p):
        for load in loads(p):
            load.start()

    def predict(p):
        _, _, row_a, row_b, col, live = decode(p)
        both = jnp.concatenate([users[row_a], users[row_b]], axis=0)
        predicted = lax.dot_general(both, items[col], (((1,), (1,)), ((), ())), preferred_element_type=jnp.float32)
        misfit = rated[lax.rem(p - low, DEPTH)].astype(jnp.float32) - predicted
        rows = lax.broadcasted_iota(jnp.int32, (2 * tile, 1), 0)
        return jnp.where(rows < tile * live, misfit, 0.0).astype(jnp.bfloat16)

    def add_grads(p, misfit):
        _, _, row_a, row_b, col, _ = decode(p)
        to_user = jnp.dot(misfit, items[col], preferred_element_type=jnp.float32)
        both = jnp.concatenate([users[row_a], users[row_b]], axis=0)
        grad_item[col] += lax.dot_general(misfit, both, (((0,), (0,)), ((), ())), preferred_element_type=jnp.float32)
        grad_user[row_a] += to_user[:tile]
        grad_user[row_b] += to_user[tile:]

    def await_group(p):
        for j in range(GROUP):
            for load in loads(p + j):
                load.wait()

    def issue_group(step):
        @pl.when(step < steps)
        def _():
            for j in range(GROUP):
                issue(low + step * GROUP + j)

    piece_loads = [
        pltpu.make_async_copy(piece_in[i], items.at[pl.ds(i * per, per)], piece_sem.at[i]) for i in range(pieces)
    ]
    for load in piece_loads:
        load.start()
    for step in range(DEPTH // GROUP):
        issue_group(step)
    grad_user[...] = jnp.zeros_like(grad_user)
    grad_item[...] = jnp.zeros_like(grad_item)
    for load in piece_loads:
        load.wait()

    @pl.when(steps > 0)
    def _():
        await_group(low)
        for j in range(GROUP):
            misfits[j] = predict(low + j)
        issue_group(DEPTH // GROUP)

        def advance(step, carry):
            p = low + step * GROUP
            held = [misfits[j] for j in range(GROUP)]
            await_group(p + GROUP)
            following = [predict(p + GROUP + j) for j in range(GROUP)]
            for j in range(GROUP):
                add_grads(p + j, held[j])
            for j in range(GROUP):
                misfits[j] = following[j]
            issue_group(step + 1 + DEPTH // GROUP)
            return carry

        lax.fori_loop(0, steps - 1, advance, 0)
        for j in range(GROUP):
            add_grads(high - GROUP + j, misfits[j])

    stores = [pltpu.make_async_copy(grad_user, grad_user_out, out_sem.at[pieces])]
    for i in range(pieces):
        stores.append(
            pltpu.make_async_copy(grad_item.at[pl.ds(i * per, per)], grad_item_out[i], out_sem.at[i])
        )
    for store in stores:
        store.start()
    for store in stores:
        store.wait()


def tile_grads(section, first_run, last_run, span, plan, ratings, users, pieces):
    pairs, starts = plan
    count = len(pieces)
    per, tile, width = pieces[0].shape
    user_tiles = users.shape[0]
    bits = widths(ratings.shape[1], user_tiles, span * (starts.shape[0] - 1))
    busy = ratings.shape[1] * 3 // 4
    f32 = jnp.float32
    return pl.pallas_call(
        functools.partial(grads_kernel, section, first_run, last_run, span, bits, count),
        out_shape=[jax.ShapeDtypeStruct((user_tiles, tile, width), f32)]
        + [jax.ShapeDtypeStruct((per, tile, width), f32)] * count,
        in_specs=[IN_SMEM, IN_SMEM, ANY, IN_VMEM] + [ANY] * count,
        out_specs=[ANY] * (1 + count),
        scratch_shapes=[
            pltpu.VMEM((count * per, tile, width), jnp.bfloat16),
            pltpu.VMEM((DEPTH, 2 * tile, tile), jnp.bfloat16),
            pltpu.VMEM((GROUP, 2 * tile, tile), jnp.bfloat16),
            pltpu.VMEM((user_tiles, tile, width), f32),
            pltpu.VMEM((count * per, tile, width), f32),
            pltpu.SemaphoreType.DMA((DEPTH, 2)),
            pltpu.SemaphoreType.DMA((count,)),
            pltpu.SemaphoreType.DMA((count + 1,)),
        ],
        compiler_params=pltpu.CompilerParams(vmem_limit_bytes=VMEM_LIMIT),
        cost_estimate=pl.CostEstimate(
            flops=busy * 6 * tile * tile * width,
            bytes_accessed=busy * tile * tile * 2 + user_tiles * tile * width * 8,
            transcendentals=0,
        ),
    )(pairs, starts, ratings, users, *pieces)


def coded_shape(per, tile, width):
    return jax.ShapeDtypeStruct((per * tile + SCALE_ROWS, width), jnp.int16)


def encode(blocks, out):
    per = len(blocks)
    tile, width = blocks[0].shape
    row = lax.broadcasted_iota(jnp.int32, (SCALE_ROWS, width), 0)
    powers = jnp.zeros((SCALE_ROWS, width), jnp.int32)
    for t, block in enumerate(blocks):
        largest = jnp.max(jnp.abs(block), axis=0, keepdims=True)
        power = jnp.ceil(jnp.log2(jnp.maximum(largest, 1e-20)))
        scaled = jnp.round(block * jnp.exp2(15.0 - power))
        out[pl.ds(t * tile, tile)] = jnp.clip(scaled, -32767.0, 32767.0).astype(jnp.int32).astype(jnp.int16)
        powers = jnp.where(row == t, power.astype(jnp.int32), powers)
    out[pl.ds(per * tile, SCALE_ROWS)] = powers.astype(jnp.int16)


def decoded(ref, t, tile, per):
    powers = ref[pl.ds(per * tile, SCALE_ROWS)].astype(jnp.int32).astype(jnp.float32)
    unit = jnp.exp2(powers[t : t + 1] - 15.0)
    return ref[pl.ds(t * tile, tile)].astype(jnp.int32).astype(jnp.float32) * unit


def join_kernel(mine, other, out):
    encode([mine[t] + other[t] for t in range(mine.shape[0])], out)


def join(mine, other):
    return pl.pallas_call(
        join_kernel,
        out_shape=coded_shape(*mine.shape),
        in_specs=[IN_VMEM] * 2,
        out_specs=IN_VMEM,
        compiler_params=pltpu.CompilerParams(vmem_limit_bytes=VMEM_LIMIT),
    )(mine, other)


def owner_sum(mine, other, coded, t):
    per, tile, _ = mine.shape
    total = mine[t] + other[t]
    for ref in coded:
        total = total + decoded(ref, t, tile, per)
    return total


def update_kernel(power, mine, other, *refs):
    *coded, factors, noise, new, new_bf = refs
    for t in range(mine.shape[0]):
        step = HALF_STEP * power * owner_sum(mine, other, coded, t) + ROOT_STEP * noise[t].astype(jnp.float32)
        after = factors[t] - HALF_STEP * PRIOR * factors[t] + step
        new[t] = after
        new_bf[t] = after.astype(jnp.bfloat16)


def delta_kernel(power, mine, other, *refs):
    *coded, noise, out = refs
    steps = []
    for t in range(mine.shape[0]):
        steps.append(HALF_STEP * power * owner_sum(mine, other, coded, t) + ROOT_STEP * noise[t].astype(jnp.float32))
    encode(steps, out)


def arrive_kernel(coded, factors, new, new_bf):
    per, tile, _ = factors.shape
    for t in range(per):
        after = factors[t] - HALF_STEP * PRIOR * factors[t] + decoded(coded, t, tile, per)
        new[t] = after
        new_bf[t] = after.astype(jnp.bfloat16)


def in_vmem(kernel, out_shape, *operands):
    return pl.pallas_call(
        kernel,
        out_shape=out_shape,
        in_specs=[IN_VMEM] * len(operands),
        out_specs=jax.tree.map(lambda _: IN_VMEM, out_shape),
        compiler_params=pltpu.CompilerParams(vmem_limit_bytes=VMEM_LIMIT),
    )(*operands)


def body(u_factors, v_factors, ratings, tile_rows, tile_cols, tile_counts, u_noise, v_noise):
    tile = ratings.shape[-1]
    sections = ratings.shape[2]
    width = u_factors.shape[1]
    peers = lax.axis_size("user")
    power = float(lax.axis_size("item"))
    me = lax.axis_index("user")
    users = u_factors.reshape(-1, tile, width)
    items = v_factors.reshape(-1, tile, width)
    per = items.shape[0]
    item_tiles = peers * per
    span = item_tiles
    ratings = ratings.reshape(ratings.shape[2:])
    u_noise = u_noise.reshape(sections, *users.shape)
    v_noise = v_noise.reshape(sections, *items.shape)
    pair = (
        jax.ShapeDtypeStruct(items.shape, jnp.float32),
        jax.ShapeDtypeStruct(items.shape, jnp.bfloat16),
    )
    plans = [
        pair_plan(
            tile_rows[0, 0, s], tile_cols[0, 0, s], tile_counts[0, 0, s], me, users.shape[0], item_tiles, per, span
        )
        for s in range(sections)
    ]
    items_bf = items.astype(jnp.bfloat16)
    for section in range(sections):
        sent = shifted(items_bf, "item", section) if section else items_bf
        pieces = [sent] + [swapped(sent, "user", d) for d in range(2, peers, 2)]
        pieces = [p for even in pieces for p in (even, swapped(even, "user", 1))]
        grad_user, *grads = tile_grads(
            section, 0, 1, span, plans[section], ratings, users.astype(jnp.bfloat16), pieces
        )
        mine = grads[0::2]
        other = [swapped(g, "user", 1) for g in grads[1::2]]
        coded = [swapped(join(mine[d], other[d]), "user", 2 * d) for d in range(1, peers // 2)]
        if section == 0:
            items, items_bf = in_vmem(
                functools.partial(update_kernel, power), pair, mine[0], other[0], *coded, items, v_noise[section]
            )
        else:
            delta = in_vmem(
                functools.partial(delta_kernel, power),
                coded_shape(*items.shape),
                mine[0],
                other[0],
                *coded,
                v_noise[section],
            )
            items, items_bf = in_vmem(arrive_kernel, pair, shifted(delta, "item", -section), items)
        users = (
            users
            + HALF_STEP * (power * grad_user - PRIOR * users)
            + ROOT_STEP * u_noise[section].astype(jnp.float32)
        )
    return (users.reshape(u_factors.shape), items.reshape(v_factors.shape))


def solution(mesh):
    placed = (
        P(("user", "item"), None),
        P(("item", "user"), None),
        P("user", "item", None, None, None, None),
        P("user", "item", None, None),
        P("user", "item", None, None),
        P("user", "item", None),
        P(None, ("user", "item"), None),
        P(None, ("item", "user"), None),
    )
    return jax.shard_map(
        body,
        mesh=mesh,
        in_specs=placed,
        out_specs=(P(("user", "item"), None), P(("item", "user"), None)),
        check_vma=False,
    )
```

```python
import functools
import math

import jax
import jax.numpy as jnp
from jax import lax
from jax.experimental import pallas as pl
from jax.experimental.pallas import tpu as pltpu
from jax.sharding import PartitionSpec as P

HALF_STEP = 0.002
ROOT_STEP = math.sqrt(0.004)
PRIOR = 25.0
GROUP = 4
SCALE_ROWS = 16
SMALL_LIMIT = 12 * 2**20
SCALE_STEPS = 128.0

ANY = pl.BlockSpec(memory_space=pl.ANY)
IN_VMEM = pl.BlockSpec(memory_space=pltpu.VMEM)
IN_SMEM = pl.BlockSpec(memory_space=pltpu.SMEM)


def shifted(x, axis, by):
    peers = lax.axis_size(axis)
    return lax.ppermute(x, axis, [(i, (i + by) % peers) for i in range(peers)])


def swapped(x, axis, mask):
    peers = lax.axis_size(axis)
    return lax.ppermute(x, axis, [(i, i ^ mask) for i in range(peers)])


def widths(slots, user_tiles, item_tiles):
    bits = tuple(max(1, (n - 1).bit_length()) for n in (slots, user_tiles, item_tiles))
    assert 2 * bits[0] + 2 * bits[1] + bits[2] + 2 <= 31
    return bits


def pair_plan(rows, cols, count, me, user_tiles, item_tiles, per, span):
    slots = rows.shape[0]
    slot_bits, row_bits, col_bits = widths(slots, user_tiles, item_tiles)
    place = ((cols // per) ^ me) * per + cols % per
    n = jnp.arange(slots, dtype=jnp.int32)
    live = n < count
    same = (place[:, None] == place[None, :]) & live[None, :]
    rank = jnp.sum(same & (rows[None, :] < rows[:, None]), axis=1, dtype=jnp.int32)
    opens = live & (rank % 2 == 0)
    run = place // span
    runs = item_tiles // span
    run_ids = jnp.arange(runs, dtype=jnp.int32)
    ahead = (place[None, :] < place[:, None]) & (run[None, :] == run[:, None]) & opens[None, :]
    within = jnp.sum(ahead, axis=1, dtype=jnp.int32)
    size = jnp.sum((run[None, :] == run_ids[:, None]) & opens[None, :], axis=1, dtype=jnp.int32)
    size = (size + GROUP - 1) // GROUP * GROUP
    edges = jnp.arange(runs + 1, dtype=jnp.int32)
    starts = jnp.sum(jnp.where(run_ids[None, :] < edges[:, None], size[None, :], 0), axis=1, dtype=jnp.int32)
    base = jnp.sum(jnp.where(run_ids[None, :] < run[:, None], size[None, :], 0), axis=1, dtype=jnp.int32)
    where = base + within + rank // 2
    col_at = 2 * slot_bits + 2 * row_bits
    one = 1 << (col_at + col_bits)
    first = n | (rows << (2 * slot_bits)) | (place << col_at)
    second = (n << slot_bits) | (rows << (2 * slot_bits + row_bits))
    word = jnp.where(live, jnp.where(rank % 2 == 0, first, second) + one, 0)
    words = jnp.arange((slots + item_tiles) // 2 + runs * GROUP, dtype=jnp.int32)[:, None]
    pairs = jnp.sum(jnp.where(where[None, :] == words, word[None, :], 0), axis=1, dtype=jnp.int32)
    unused = jnp.sum(words >= starts[None, 1:], axis=1, dtype=jnp.int32) * span
    unused = jnp.minimum(unused, item_tiles - 1) << col_at
    return jnp.where(pairs == 0, unused, pairs), starts


def decode_word(word, bits, first_col):
    slot_bits, row_bits, col_bits = bits
    fields = []
    for width in (slot_bits, slot_bits, row_bits, row_bits, col_bits):
        fields.append(word & ((1 << width) - 1))
        word = word >> width
    fields[4] -= first_col
    return (*fields, word)


def fetch_kernel(section, lump, counts, ratings, out, sem):
    lumps = lax.div(counts[section] + lump - 1, lump)

    def load(i):
        part = pl.ds(i * lump, lump)
        return pltpu.make_async_copy(ratings.at[section, part], out.at[part], sem.at[i])

    lax.fori_loop(0, lumps, lambda i, c: (load(i).start(), c)[1], 0)
    lax.fori_loop(0, lumps, lambda i, c: (load(i).wait(), c)[1], 0)


def fetch(section, counts, ratings):
    slots = ratings.shape[1]
    lump = math.gcd(slots, 16)
    return pl.pallas_call(
        functools.partial(fetch_kernel, section, lump),
        out_shape=jax.ShapeDtypeStruct(ratings.shape[1:], ratings.dtype),
        in_specs=[IN_SMEM, ANY],
        out_specs=IN_VMEM,
        scratch_shapes=[pltpu.SemaphoreType.DMA((slots // lump,))],
        compiler_params=pltpu.CompilerParams(vmem_limit_bytes=SMALL_LIMIT),
        cost_estimate=pl.CostEstimate(flops=0, bytes_accessed=slots * 2**15, transcendentals=0),
    )(counts, ratings)


def items_kernel(run, span, bits, pairs, starts, rated, users, even, odd, out_even, out_odd, misfits, items, grad):
    per = even.shape[0]
    tile = users.shape[1]
    low, high = starts[run], starts[run + 1]
    steps = lax.div(high - low, GROUP)
    for t in range(per):
        items[t] = even[t]
        items[per + t] = odd[t]
    grad[...] = jnp.zeros_like(grad)

    def decode(p):
        return decode_word(pairs[p], bits, run * span)

    def users_of(row_a, row_b):
        return jnp.concatenate([users[row_a], users[row_b]], axis=0)

    def predict(p):
        slot_a, slot_b, row_a, row_b, col, live = decode(p)
        predicted = lax.dot_general(
            users_of(row_a, row_b), items[col], (((1,), (1,)), ((), ())), preferred_element_type=jnp.float32
        )
        given = jnp.concatenate([rated[slot_a], rated[slot_b]], axis=0).astype(jnp.float32)
        rows = lax.broadcasted_iota(jnp.int32, (2 * tile, 1), 0)
        return jnp.where(rows < tile * live, given - predicted, 0.0).astype(jnp.bfloat16)

    def add_grad(p, misfit):
        _, _, row_a, row_b, col, _ = decode(p)
        grad[col] += lax.dot_general(
            misfit, users_of(row_a, row_b), (((0,), (0,)), ((), ())), preferred_element_type=jnp.float32
        )

    @pl.when(steps > 0)
    def _():
        for j in range(GROUP):
            misfits[j] = predict(low + j)

        def advance(step, carry):
            at = step * GROUP
            held = [misfits[at + j] for j in range(GROUP)]
            following = [predict(low + at + GROUP + j) for j in range(GROUP)]
            for j in range(GROUP):
                add_grad(low + at + j, held[j])
            for j in range(GROUP):
                misfits[at + GROUP + j] = following[j]
            return carry

        lax.fori_loop(0, steps - 1, advance, 0)
        for j in range(GROUP):
            add_grad(high - GROUP + j, misfits[high - low - GROUP + j])

    for t in range(per):
        out_even[t] = grad[t]
        out_odd[t] = grad[per + t]


def item_grads(run, span, bits, plan, rated, users, even, odd):
    per, tile, width = even.shape
    held = span * ((users.shape[0] + 1) // 2)
    held = (min(held, (rated.shape[0] + span) // 2) + GROUP - 1) // GROUP * GROUP
    f32 = jnp.float32
    return pl.pallas_call(
        functools.partial(items_kernel, run, span, bits),
        out_shape=[jax.ShapeDtypeStruct((per, tile, width), f32)] * 2
        + [jax.ShapeDtypeStruct((held, 2 * tile, tile), jnp.bfloat16)],
        in_specs=[IN_SMEM, IN_SMEM] + [IN_VMEM] * 4,
        out_specs=[IN_VMEM] * 3,
        scratch_shapes=[pltpu.VMEM((span, tile, width), jnp.bfloat16), pltpu.VMEM((span, tile, width), f32)],
        compiler_params=pltpu.CompilerParams(vmem_limit_bytes=SMALL_LIMIT),
        cost_estimate=pl.CostEstimate(flops=3 * 10**9, bytes_accessed=2**20, transcendentals=0),
    )(*plan, rated, users, even, odd)


def users_kernel(power, span, bits, runs, pairs, starts, *refs):
    pieces = refs[: 2 * runs]
    misfits = refs[2 * runs : 3 * runs]
    factors, noise, new, new_bf, items, grad = refs[3 * runs :]
    per = pieces[0].shape[0]
    tile = factors.shape[1]
    for i, piece in enumerate(pieces):
        for t in range(per):
            items[i * per + t] = piece[t]
    grad[...] = jnp.zeros_like(grad)
    for run in range(runs):
        low = starts[run]

        def advance(step, carry, low=low, held=misfits[run]):
            for j in range(GROUP):
                i = step * GROUP + j
                _, _, row_a, row_b, col, _ = decode_word(pairs[low + i], bits, 0)
                part = jnp.dot(held[i], items[col], preferred_element_type=jnp.float32)
                grad[row_a] += part[:tile]
                grad[row_b] += part[tile:]
            return carry

        lax.fori_loop(0, lax.div(starts[run + 1] - low, GROUP), advance, 0)

    def finish(t, carry):
        before = factors[t]
        after = (
            before + HALF_STEP * (power * grad[t] - PRIOR * before) + ROOT_STEP * noise[t].astype(jnp.float32)
        )
        new[t] = after
        new_bf[t] = after.astype(jnp.bfloat16)
        return carry

    lax.fori_loop(0, factors.shape[0], finish, 0)


def user_step(power, span, bits, plan, pieces, misfits, factors, noise):
    shape = factors.shape
    per, tile, width = pieces[0].shape
    f32 = jnp.float32
    return pl.pallas_call(
        functools.partial(users_kernel, power, span, bits, len(misfits)),
        out_shape=[jax.ShapeDtypeStruct(shape, f32), jax.ShapeDtypeStruct(shape, jnp.bfloat16)],
        in_specs=[IN_SMEM, IN_SMEM] + [IN_VMEM] * (len(pieces) + len(misfits) + 2),
        out_specs=[IN_VMEM] * 2,
        scratch_shapes=[pltpu.VMEM((len(pieces) * per, tile, width), jnp.bfloat16), pltpu.VMEM(shape, f32)],
        compiler_params=pltpu.CompilerParams(vmem_limit_bytes=SMALL_LIMIT),
        cost_estimate=pl.CostEstimate(flops=8 * 10**9, bytes_accessed=2**20, transcendentals=0),
    )(*plan, *pieces, *misfits, factors, noise)


def coded_shape(per, tile, width):
    return jax.ShapeDtypeStruct((per * tile + SCALE_ROWS, width), jnp.int16)


def encode(blocks, out):
    per = len(blocks)
    tile, width = blocks[0].shape
    row = lax.broadcasted_iota(jnp.int32, (SCALE_ROWS, width), 0)
    powers = jnp.zeros((SCALE_ROWS, width), jnp.int32)
    for t, block in enumerate(blocks):
        largest = jnp.max(jnp.abs(block), axis=0, keepdims=True)
        power = jnp.ceil(SCALE_STEPS * jnp.log2(jnp.maximum(largest, 1e-20)))
        scaled = jnp.round(block * jnp.exp2(15.0 - power / SCALE_STEPS))
        out[pl.ds(t * tile, tile)] = jnp.clip(scaled, -32767.0, 32767.0).astype(jnp.int32).astype(jnp.int16)
        powers = jnp.where(row == t, power.astype(jnp.int32), powers)
    out[pl.ds(per * tile, SCALE_ROWS)] = powers.astype(jnp.int16)


def decoded(ref, t, tile, per):
    powers = ref[pl.ds(per * tile, SCALE_ROWS)].astype(jnp.int32).astype(jnp.float32)
    unit = jnp.exp2(powers[t : t + 1] / SCALE_STEPS - 15.0)
    return ref[pl.ds(t * tile, tile)].astype(jnp.int32).astype(jnp.float32) * unit


def join_kernel(mine, other, out):
    encode([mine[t] + other[t] for t in range(mine.shape[0])], out)


def join(mine, other):
    return pl.pallas_call(
        join_kernel,
        out_shape=coded_shape(*mine.shape),
        in_specs=[IN_VMEM] * 2,
        out_specs=IN_VMEM,
        compiler_params=pltpu.CompilerParams(vmem_limit_bytes=SMALL_LIMIT),
    )(mine, other)


def owner_sum(mine, other, coded, t):
    per, tile, _ = mine.shape
    total = mine[t] + other[t]
    for ref in coded:
        total = total + decoded(ref, t, tile, per)
    return total


def update_kernel(power, mine, other, *refs):
    *coded, factors, noise, new, new_bf = refs
    for t in range(mine.shape[0]):
        step = HALF_STEP * power * owner_sum(mine, other, coded, t) + ROOT_STEP * noise[t].astype(jnp.float32)
        after = factors[t] - HALF_STEP * PRIOR * factors[t] + step
        new[t] = after
        new_bf[t] = after.astype(jnp.bfloat16)


def delta_kernel(power, mine, other, *refs):
    *coded, noise, out = refs
    steps = []
    for t in range(mine.shape[0]):
        steps.append(HALF_STEP * power * owner_sum(mine, other, coded, t) + ROOT_STEP * noise[t].astype(jnp.float32))
    encode(steps, out)


def arrive_kernel(coded, factors, new, new_bf):
    per, tile, _ = factors.shape
    for t in range(per):
        after = factors[t] - HALF_STEP * PRIOR * factors[t] + decoded(coded, t, tile, per)
        new[t] = after
        new_bf[t] = after.astype(jnp.bfloat16)


def in_vmem(kernel, out_shape, *operands):
    return pl.pallas_call(
        kernel,
        out_shape=out_shape,
        in_specs=[IN_VMEM] * len(operands),
        out_specs=jax.tree.map(lambda _: IN_VMEM, out_shape),
        compiler_params=pltpu.CompilerParams(vmem_limit_bytes=SMALL_LIMIT),
    )(*operands)


def body(u_factors, v_factors, ratings, tile_rows, tile_cols, tile_counts, u_noise, v_noise):
    tile = ratings.shape[-1]
    sections = ratings.shape[2]
    width = u_factors.shape[1]
    peers = lax.axis_size("user")
    power = float(lax.axis_size("item"))
    me = lax.axis_index("user")
    users = u_factors.reshape(-1, tile, width)
    items = v_factors.reshape(-1, tile, width)
    per = items.shape[0]
    item_tiles = peers * per
    span = 2 * per
    runs = item_tiles // span
    ratings = ratings.reshape(ratings.shape[2:])
    counts = tile_counts.reshape(sections)
    u_noise = u_noise.reshape(sections, *users.shape)
    v_noise = v_noise.reshape(sections, *items.shape)
    bits = widths(ratings.shape[1], users.shape[0], item_tiles)
    pair = (
        jax.ShapeDtypeStruct(items.shape, jnp.float32),
        jax.ShapeDtypeStruct(items.shape, jnp.bfloat16),
    )
    items_bf = items.astype(jnp.bfloat16)
    users_bf = users.astype(jnp.bfloat16)
    for section in range(sections):
        sent = shifted(items_bf, "item", section) if section else items_bf
        evens = [sent] + [swapped(sent, "user", 2 * d) for d in range(1, runs)]
        odds = [swapped(even, "user", 1) for even in evens]
        plan = pair_plan(
            tile_rows[0, 0, section],
            tile_cols[0, 0, section],
            counts[section],
            me,
            users.shape[0],
            item_tiles,
            per,
            span,
        )
        rated = fetch(section, counts, ratings)
        mine, other, misfits = [], [], []
        for run in range(runs):
            even_grad, odd_grad, held = item_grads(run, span, bits, plan, rated, users_bf, evens[run], odds[run])
            mine.append(even_grad)
            other.append(swapped(odd_grad, "user", 1))
            misfits.append(held)
        coded = [swapped(join(mine[d], other[d]), "user", 2 * d) for d in range(1, runs)]
        if section == 0:
            items, items_bf = in_vmem(
                functools.partial(update_kernel, power), pair, mine[0], other[0], *coded, items, v_noise[section]
            )
        else:
            delta = in_vmem(
                functools.partial(delta_kernel, power),
                coded_shape(*items.shape),
                mine[0],
                other[0],
                *coded,
                v_noise[section],
            )
            items, items_bf = in_vmem(arrive_kernel, pair, shifted(delta, "item", -section), items)
        pieces = [piece for both in zip(evens, odds) for piece in both]
        users, users_bf = user_step(power, span, bits, plan, pieces, misfits, users, u_noise[section])
    return (users.reshape(u_factors.shape), items.reshape(v_factors.shape))


def solution(mesh):
    placed = (
        P(("user", "item"), None),
        P(("item", "user"), None),
        P("user", "item", None, None, None, None),
        P("user", "item", None, None),
        P("user", "item", None, None),
        P("user", "item", None),
        P(None, ("user", "item"), None),
        P(None, ("item", "user"), None),
    )
    return jax.shard_map(
        body,
        mesh=mesh,
        in_specs=placed,
        out_specs=(P(("user", "item"), None), P(("item", "user"), None)),
        check_vma=False,
    )
```

```python
import functools
import math

import jax
import jax.numpy as jnp
from jax import lax
from jax.experimental import pallas as pl
from jax.experimental.pallas import tpu as pltpu
from jax.sharding import PartitionSpec as P

HALF_STEP = 0.002
ROOT_STEP = math.sqrt(0.004)
PRIOR = 25.0
GROUP = 4
SCALE_ROWS = 16
SMALL_LIMIT = 12 * 2**20
SCALE_STEPS = 128.0

ANY = pl.BlockSpec(memory_space=pl.ANY)
IN_HBM = pl.BlockSpec(memory_space=pltpu.HBM)
IN_VMEM = pl.BlockSpec(memory_space=pltpu.VMEM)
IN_SMEM = pl.BlockSpec(memory_space=pltpu.SMEM)


def shifted(x, axis, by):
    peers = lax.axis_size(axis)
    return lax.ppermute(x, axis, [(i, (i + by) % peers) for i in range(peers)])


def swapped(x, axis, mask):
    peers = lax.axis_size(axis)
    return lax.ppermute(x, axis, [(i, i ^ mask) for i in range(peers)])


def widths(slots, user_tiles, item_tiles):
    bits = tuple(max(1, (n - 1).bit_length()) for n in (slots, user_tiles, item_tiles))
    assert 2 * bits[0] + 2 * bits[1] + bits[2] + 2 <= 31
    return bits


def total(x, axis):
    return jnp.sum(x.astype(jnp.float32), axis=axis, keepdims=True).astype(jnp.int32)


def plan_kernel(section, bits, per, span, runs, me, counts, lists, pairs, starts):
    slot_bits, row_bits, col_bits = bits
    side = lists.shape[-1]
    shape = (side, side)
    count = counts[section]
    along = lax.broadcasted_iota(jnp.int32, shape, 1)
    down = lax.broadcasted_iota(jnp.int32, shape, 0)
    row_along = jnp.broadcast_to(lists[section, 0:1], shape)
    place_along = jnp.broadcast_to(lists[section, 1:2] ^ (me[0] * per), shape)
    key = (place_along << row_bits | row_along).astype(jnp.float32).T.astype(jnp.int32)
    row_down = key & ((1 << row_bits) - 1)
    place_down = key >> row_bits
    span_bits = span.bit_length() - 1
    run_along, run_down = place_along >> span_bits, place_down >> span_bits
    live_along, live_down = along < count, down < count
    same = place_along == place_down
    rank_down = total(same & live_along & (row_along < row_down), 1)
    rank_along = total(same & live_down & (row_down < row_along), 0)
    opens = live_along & ((rank_along & 1) == 0)
    within = total(opens & (run_along == run_down) & (place_along < place_down), 1)
    base = jnp.zeros((side, 1), jnp.int32)
    begins = jnp.zeros((1, side), jnp.int32)
    unused = jnp.zeros((1, side), jnp.int32)
    ahead = jnp.zeros((1, 1), jnp.int32)
    for run in range(runs):
        size = total(opens[0:1] & (run_along[0:1] == run), 1)
        size = (size + GROUP - 1) & ~(GROUP - 1)
        base += jnp.where(run_down[:, 0:1] > run, size, 0)
        begins += jnp.where(along[0:1] > run, size, 0)
        ahead += size
        unused += jnp.where(along[0:1] >= ahead, span, 0)
    where = base + within + (rank_down >> 1)
    col_at = 2 * slot_bits + 2 * row_bits
    odd = rank_down & 1
    n, row, place = down[:, 0:1], row_down[:, 0:1], place_down[:, 0:1]
    word = jnp.where(odd == 0, n, n << slot_bits)
    word += jnp.where(odd == 0, row, row << row_bits) << (2 * slot_bits)
    word += (jnp.where(odd == 0, place, 0) << col_at) + (1 << (col_at + col_bits))
    word = jnp.broadcast_to(word, shape)
    hit = (where == along) & live_down
    low = total(jnp.where(hit, word & 0xFFFF, 0), 0)
    high = total(jnp.where(hit, word >> 16, 0), 0)
    listed = (high << 16) | low
    unused = jnp.minimum(unused, span * runs - 1) << col_at
    pairs[...] = jnp.where(listed == 0, unused, listed)
    starts[...] = begins


def pair_plan(section, bits, per, span, runs, me, counts, lists):
    side = lists.shape[-1]
    return pl.pallas_call(
        functools.partial(plan_kernel, section, bits, per, span, runs),
        out_shape=[jax.ShapeDtypeStruct((1, side), jnp.int32)] * 2,
        in_specs=[IN_SMEM, IN_SMEM, IN_VMEM],
        out_specs=[IN_VMEM] * 2,
        compiler_params=pltpu.CompilerParams(vmem_limit_bytes=SMALL_LIMIT),
        cost_estimate=pl.CostEstimate(flops=10**9, bytes_accessed=2**12, transcendentals=0),
    )(me, counts, lists)


def decode_word(word, bits, first_col):
    slot_bits, row_bits, col_bits = bits
    fields = []
    for width in (slot_bits, slot_bits, row_bits, row_bits, col_bits):
        fields.append(word & ((1 << width) - 1))
        word = word >> width
    fields[4] -= first_col
    return (*fields, word)


def fetch_kernel(section, lump, counts, ratings, out, sem):
    lumps = lax.div(counts[section] + lump - 1, lump)

    def load(i):
        part = pl.ds(i * lump, lump)
        return pltpu.make_async_copy(ratings.at[section, part], out.at[part], sem.at[i])

    lax.fori_loop(0, lumps, lambda i, c: (load(i).start(), c)[1], 0)
    lax.fori_loop(0, lumps, lambda i, c: (load(i).wait(), c)[1], 0)


def fetch(section, counts, ratings):
    slots = ratings.shape[1]
    lump = math.gcd(slots, 16)
    return pl.pallas_call(
        functools.partial(fetch_kernel, section, lump),
        out_shape=jax.ShapeDtypeStruct(ratings.shape[1:], ratings.dtype),
        in_specs=[IN_SMEM, IN_HBM],
        out_specs=IN_VMEM,
        scratch_shapes=[pltpu.SemaphoreType.DMA((slots // lump,))],
        compiler_params=pltpu.CompilerParams(vmem_limit_bytes=SMALL_LIMIT),
        cost_estimate=pl.CostEstimate(flops=0, bytes_accessed=slots * 2**15, transcendentals=0),
    )(counts, ratings)


def items_kernel(run, span, bits, pairs, starts, rated, users, even, odd, *refs):
    out_even, out_odd, misfits, items, grad = refs[-5:]
    per = even.shape[0]
    tile = users.shape[1]
    low, high = starts[0, run], starts[0, run + 1]
    steps = lax.div(high - low, GROUP)
    for t in range(per):
        items[t] = even[t]
        items[per + t] = odd[t]
    grad[...] = jnp.zeros_like(grad)

    def decode(p):
        return decode_word(pairs[0, p], bits, run * span)

    def users_of(row_a, row_b):
        return jnp.concatenate([users[row_a], users[row_b]], axis=0)

    def predict(p):
        slot_a, slot_b, row_a, row_b, col, live = decode(p)
        predicted = lax.dot_general(
            users_of(row_a, row_b), items[col], (((1,), (1,)), ((), ())), preferred_element_type=jnp.float32
        )
        given = jnp.concatenate([rated[slot_a], rated[slot_b]], axis=0).astype(jnp.float32)
        rows = lax.broadcasted_iota(jnp.int32, (2 * tile, 1), 0)
        return jnp.where(rows < tile * live, given - predicted, 0.0).astype(jnp.bfloat16)

    def add_grad(p, misfit):
        _, _, row_a, row_b, col, _ = decode(p)
        grad[col] += lax.dot_general(
            misfit, users_of(row_a, row_b), (((0,), (0,)), ((), ())), preferred_element_type=jnp.float32
        )

    @pl.when(steps > 0)
    def _():
        for j in range(GROUP):
            misfits[j] = predict(low + j)

        def advance(step, carry):
            at = step * GROUP
            held = [misfits[at + j] for j in range(GROUP)]
            following = [predict(low + at + GROUP + j) for j in range(GROUP)]
            for j in range(GROUP):
                add_grad(low + at + j, held[j])
            for j in range(GROUP):
                misfits[at + GROUP + j] = following[j]
            return carry

        lax.fori_loop(0, steps - 1, advance, 0)
        for j in range(GROUP):
            add_grad(high - GROUP + j, misfits[high - low - GROUP + j])

    for t in range(per):
        out_even[t] = grad[t]
        out_odd[t] = grad[per + t]


def item_grads(run, span, bits, plan, rated, users, even, odd, after):
    per, tile, width = even.shape
    held = span * ((users.shape[0] + 1) // 2)
    held = (min(held, (rated.shape[0] + span) // 2) + GROUP - 1) // GROUP * GROUP
    f32 = jnp.float32
    return pl.pallas_call(
        functools.partial(items_kernel, run, span, bits),
        out_shape=[jax.ShapeDtypeStruct((per, tile, width), f32)] * 2
        + [jax.ShapeDtypeStruct((held, 2 * tile, tile), jnp.bfloat16)],
        in_specs=[IN_SMEM, IN_SMEM] + [IN_VMEM] * 4 + [ANY] * len(after),
        out_specs=[IN_VMEM] * 3,
        scratch_shapes=[pltpu.VMEM((span, tile, width), jnp.bfloat16), pltpu.VMEM((span, tile, width), f32)],
        compiler_params=pltpu.CompilerParams(vmem_limit_bytes=SMALL_LIMIT),
        cost_estimate=pl.CostEstimate(flops=3 * 10**9, bytes_accessed=2**20, transcendentals=0),
    )(*plan, rated, users, even, odd, *after)


def add_user_grads(bits, first_run, pairs, starts, pieces, misfits, items, grad):
    per, tile = pieces[0].shape[:2]
    first_col = 2 * per * first_run
    for i, piece in enumerate(pieces):
        for t in range(per):
            items[i * per + t] = piece[t]
    for k, held in enumerate(misfits):
        low = starts[0, first_run + k]

        def advance(step, carry, low=low, held=held):
            for j in range(GROUP):
                i = step * GROUP + j
                _, _, row_a, row_b, col, _ = decode_word(pairs[0, low + i], bits, first_col)
                part = jnp.dot(held[i], items[col], preferred_element_type=jnp.float32)
                grad[row_a] += part[:tile]
                grad[row_b] += part[tile:]
            return carry

        lax.fori_loop(0, lax.div(starts[0, first_run + k + 1] - low, GROUP), advance, 0)


def users_head_kernel(bits, runs, pairs, starts, *refs):
    grad, items = refs[-2:]
    grad[...] = jnp.zeros_like(grad)
    add_user_grads(bits, 0, pairs, starts, refs[: 2 * runs], refs[2 * runs : 3 * runs], items, grad)


def users_tail_kernel(power, bits, first_run, runs, pairs, starts, *refs):
    factors, noise, partial, new, new_bf, items, grad = refs[3 * runs :]
    grad[...] = partial[...]
    add_user_grads(bits, first_run, pairs, starts, refs[: 2 * runs], refs[2 * runs : 3 * runs], items, grad)

    def finish(t, carry):
        before = factors[t]
        after = (
            before + HALF_STEP * (power * grad[t] - PRIOR * before) + ROOT_STEP * noise[t].astype(jnp.float32)
        )
        new[t] = after
        new_bf[t] = after.astype(jnp.bfloat16)
        return carry

    lax.fori_loop(0, factors.shape[0], finish, 0)


def users_head(bits, plan, pieces, misfits, shape):
    per, tile, width = pieces[0].shape
    return pl.pallas_call(
        functools.partial(users_head_kernel, bits, len(misfits)),
        out_shape=jax.ShapeDtypeStruct(shape, jnp.float32),
        in_specs=[IN_SMEM, IN_SMEM] + [IN_VMEM] * (len(pieces) + len(misfits)),
        out_specs=IN_VMEM,
        scratch_shapes=[pltpu.VMEM((len(pieces) * per, tile, width), jnp.bfloat16)],
        compiler_params=pltpu.CompilerParams(vmem_limit_bytes=SMALL_LIMIT),
        cost_estimate=pl.CostEstimate(flops=6 * 10**9, bytes_accessed=2**20, transcendentals=0),
    )(*plan, *pieces, *misfits)


def users_tail(power, bits, first_run, plan, pieces, misfits, factors, noise, partial):
    shape = factors.shape
    per, tile, width = pieces[0].shape
    return pl.pallas_call(
        functools.partial(users_tail_kernel, power, bits, first_run, len(misfits)),
        out_shape=[jax.ShapeDtypeStruct(shape, jnp.float32), jax.ShapeDtypeStruct(shape, jnp.bfloat16)],
        in_specs=[IN_SMEM, IN_SMEM] + [IN_VMEM] * (len(pieces) + len(misfits) + 3),
        out_specs=[IN_VMEM] * 2,
        scratch_shapes=[
            pltpu.VMEM((len(pieces) * per, tile, width), jnp.bfloat16),
            pltpu.VMEM(shape, jnp.float32),
        ],
        compiler_params=pltpu.CompilerParams(vmem_limit_bytes=SMALL_LIMIT),
        cost_estimate=pl.CostEstimate(flops=5 * 10**9, bytes_accessed=2**20, transcendentals=0),
    )(*plan, *pieces, *misfits, factors, noise, partial)


def coded_shape(per, tile, width):
    return jax.ShapeDtypeStruct((per * tile + SCALE_ROWS, width), jnp.int16)


def encode(blocks, out):
    per = len(blocks)
    tile, width = blocks[0].shape
    row = lax.broadcasted_iota(jnp.int32, (SCALE_ROWS, width), 0)
    powers = jnp.zeros((SCALE_ROWS, width), jnp.int32)
    for t, block in enumerate(blocks):
        largest = jnp.max(jnp.abs(block), axis=0, keepdims=True)
        power = jnp.ceil(SCALE_STEPS * jnp.log2(jnp.maximum(largest, 1e-20)))
        scaled = jnp.round(block * jnp.exp2(15.0 - power / SCALE_STEPS))
        out[pl.ds(t * tile, tile)] = jnp.clip(scaled, -32767.0, 32767.0).astype(jnp.int32).astype(jnp.int16)
        powers = jnp.where(row == t, power.astype(jnp.int32), powers)
    out[pl.ds(per * tile, SCALE_ROWS)] = powers.astype(jnp.int16)


def decoded(ref, t, tile, per):
    powers = ref[pl.ds(per * tile, SCALE_ROWS)].astype(jnp.int32).astype(jnp.float32)
    unit = jnp.exp2(powers[t : t + 1] / SCALE_STEPS - 15.0)
    return ref[pl.ds(t * tile, tile)].astype(jnp.int32).astype(jnp.float32) * unit


def join_kernel(mine, other, *refs):
    out = refs[-1]
    encode([mine[t] + other[t] for t in range(mine.shape[0])], out)


def join(mine, other, after):
    return pl.pallas_call(
        join_kernel,
        out_shape=coded_shape(*mine.shape),
        in_specs=[IN_VMEM] * 2 + [ANY] * len(after),
        out_specs=IN_VMEM,
        compiler_params=pltpu.CompilerParams(vmem_limit_bytes=SMALL_LIMIT),
    )(mine, other, *after)


def owner_sum(mine, other, coded, t):
    per, tile, _ = mine.shape
    total = mine[t] + other[t]
    for ref in coded:
        total = total + decoded(ref, t, tile, per)
    return total


def update_kernel(power, mine, other, *refs):
    *coded, factors, noise, _, new, new_bf = refs
    for t in range(mine.shape[0]):
        step = HALF_STEP * power * owner_sum(mine, other, coded, t) + ROOT_STEP * noise[t].astype(jnp.float32)
        after = factors[t] - HALF_STEP * PRIOR * factors[t] + step
        new[t] = after
        new_bf[t] = after.astype(jnp.bfloat16)


def delta_kernel(power, mine, other, *refs):
    *coded, noise, _, out = refs
    steps = []
    for t in range(mine.shape[0]):
        steps.append(HALF_STEP * power * owner_sum(mine, other, coded, t) + ROOT_STEP * noise[t].astype(jnp.float32))
    encode(steps, out)


def arrive_kernel(coded, factors, new, new_bf):
    per, tile, _ = factors.shape
    for t in range(per):
        after = factors[t] - HALF_STEP * PRIOR * factors[t] + decoded(coded, t, tile, per)
        new[t] = after
        new_bf[t] = after.astype(jnp.bfloat16)


def in_vmem(kernel, out_shape, *operands, after=()):
    return pl.pallas_call(
        kernel,
        out_shape=out_shape,
        in_specs=[IN_VMEM] * len(operands) + [ANY] * len(after),
        out_specs=jax.tree.map(lambda _: IN_VMEM, out_shape),
        compiler_params=pltpu.CompilerParams(vmem_limit_bytes=SMALL_LIMIT),
    )(*operands, *after)


def body(u_factors, v_factors, ratings, tile_rows, tile_cols, tile_counts, u_noise, v_noise):
    tile = ratings.shape[-1]
    sections = ratings.shape[2]
    width = u_factors.shape[1]
    peers = lax.axis_size("user")
    power = float(lax.axis_size("item"))
    me = lax.axis_index("user").astype(jnp.int32).reshape(1)
    users = u_factors.reshape(-1, tile, width)
    items = v_factors.reshape(-1, tile, width)
    per = items.shape[0]
    item_tiles = peers * per
    span = 2 * per
    runs = item_tiles // span
    ratings = ratings.reshape(ratings.shape[2:])
    counts = tile_counts.reshape(sections)
    u_noise = u_noise.reshape(sections, *users.shape)
    v_noise = v_noise.reshape(sections, *items.shape)
    side = -(-ratings.shape[1] // 128) * 128
    lists = jnp.stack([tile_rows[0, 0], tile_cols[0, 0]], axis=1)
    lists = jnp.pad(lists, ((0, 0), (0, 0), (0, side - ratings.shape[1])))
    assert (ratings.shape[1] + item_tiles) // 2 + runs * GROUP <= side and span & (span - 1) == 0
    bits = widths(ratings.shape[1], users.shape[0], item_tiles)
    pair = (
        jax.ShapeDtypeStruct(items.shape, jnp.float32),
        jax.ShapeDtypeStruct(items.shape, jnp.bfloat16),
    )
    items_bf = items.astype(jnp.bfloat16)
    users_bf = users.astype(jnp.bfloat16)
    for section in range(sections):
        sent = shifted(items_bf, "item", section) if section else items_bf
        evens = [sent] + [swapped(sent, "user", 2 * d) for d in range(1, runs)]
        odds = [swapped(even, "user", 1) for even in evens]
        plan = pair_plan(section, bits, per, span, runs, me, counts, lists)
        rated = fetch(section, counts, ratings)
        mine, other, misfits, coded = [], [], [], []
        after = ()
        for run in range(runs):
            even_grad, odd_grad, held = item_grads(
                run, span, bits, plan, rated, users_bf, evens[run], odds[run], after
            )
            mine.append(even_grad)
            other.append(swapped(odd_grad, "user", 1))
            misfits.append(held)
            after = (even_grad,)
            if run >= 2:
                coded.append(join(mine[run - 1], other[run - 1], after))
                after = (coded[-1],)
        coded.append(join(mine[-1], other[-1], after))
        coded = [swapped(c, "user", 2 * d) for d, c in enumerate(coded, 1)]
        pieces = [piece for both in zip(evens, odds) for piece in both]
        partial = users_head(bits, plan, pieces[:-2], misfits[:-1], users.shape)
        if section == 0:
            items, items_bf = in_vmem(
                functools.partial(update_kernel, power),
                pair,
                mine[0],
                other[0],
                *coded,
                items,
                v_noise[section],
                after=(partial,),
            )
        else:
            delta = in_vmem(
                functools.partial(delta_kernel, power),
                coded_shape(*items.shape),
                mine[0],
                other[0],
                *coded,
                v_noise[section],
                after=(partial,),
            )
            items, items_bf = in_vmem(arrive_kernel, pair, shifted(delta, "item", -section), items)
        users, users_bf = users_tail(
            power, bits, runs - 1, plan, pieces[-2:], misfits[-1:], users, u_noise[section], partial
        )
    return (users.reshape(u_factors.shape), items.reshape(v_factors.shape))


def solution(mesh):
    placed = (
        P(("user", "item"), None),
        P(("item", "user"), None),
        P("user", "item", None, None, None, None),
        P("user", "item", None, None),
        P("user", "item", None, None),
        P("user", "item", None),
        P(None, ("user", "item"), None),
        P(None, ("item", "user"), None),
    )
    return jax.shard_map(
        body,
        mesh=mesh,
        in_specs=placed,
        out_specs=(P(("user", "item"), None), P(("item", "user"), None)),
        check_vma=False,
    )
```

```python
import functools
import math

import jax
import jax.numpy as jnp
from jax import lax
from jax.experimental import pallas as pl
from jax.experimental.pallas import tpu as pltpu
from jax.sharding import PartitionSpec as P

HALF_STEP = 0.002
ROOT_STEP = math.sqrt(0.004)
PRIOR = 25.0
GROUP = 4
SCALE_ROWS = 16
SMALL_LIMIT = 12 * 2**20
FETCH_LIMIT = 38 * 2**20
SCALE_STEPS = 128.0
SCALARS = 16
LONG = pl.CostEstimate(flops=4 * 10**9, bytes_accessed=2**12, transcendentals=0)
BRIEF = pl.CostEstimate(flops=10**8, bytes_accessed=2**12, transcendentals=0)

ANY = pl.BlockSpec(memory_space=pl.ANY)
IN_HBM = pl.BlockSpec(memory_space=pltpu.HBM)
IN_VMEM = pl.BlockSpec(memory_space=pltpu.VMEM)
IN_SMEM = pl.BlockSpec(memory_space=pltpu.SMEM)


def shifted(x, axis, by):
    peers = lax.axis_size(axis)
    return lax.ppermute(x, axis, [(i, (i + by) % peers) for i in range(peers)])


def swapped(x, axis, mask):
    peers = lax.axis_size(axis)
    return lax.ppermute(x, axis, [(i, i ^ mask) for i in range(peers)])


def widths(slots, user_tiles, item_tiles):
    bits = tuple(max(1, (n - 1).bit_length()) for n in (slots, user_tiles, item_tiles))
    assert 2 * bits[0] + 2 * bits[1] + bits[2] + 2 <= 31
    return bits


def total(x, axis):
    return jnp.sum(x.astype(jnp.float32), axis=axis, keepdims=True).astype(jnp.int32)


def plan_kernel(section, bits, per, span, runs, me, counts, rows, cols, words, lists):
    slot_bits, row_bits, col_bits = bits
    side = lists.shape[-1]
    slots = rows.shape[-1]
    shape = (side, side)
    count = counts[section]
    lists[...] = jnp.zeros_like(lists)
    lists[0:1, 0:slots] = rows[0, 0, section : section + 1]
    lists[1:2, 0:slots] = cols[0, 0, section : section + 1]
    along = lax.broadcasted_iota(jnp.int32, shape, 1)
    down = lax.broadcasted_iota(jnp.int32, shape, 0)
    row_along = jnp.broadcast_to(lists[0:1], shape)
    place_along = jnp.broadcast_to(lists[1:2] ^ (me[0] * per), shape)
    key = (place_along << row_bits | row_along).astype(jnp.float32).T.astype(jnp.int32)
    row_down = key & ((1 << row_bits) - 1)
    place_down = key >> row_bits
    span_bits = span.bit_length() - 1
    run_along, run_down = place_along >> span_bits, place_down >> span_bits
    live_along, live_down = along < count, down < count
    same = place_along == place_down
    rank_down = total(same & live_along & (row_along < row_down), 1)
    rank_along = total(same & live_down & (row_down < row_along), 0)
    opens = live_along & ((rank_along & 1) == 0)
    within = total(opens & (run_along == run_down) & (place_along < place_down), 1)
    base = jnp.zeros((side, 1), jnp.int32)
    begins = jnp.zeros((1, side), jnp.int32)
    unused = jnp.zeros((1, side), jnp.int32)
    ahead = jnp.zeros((1, 1), jnp.int32)
    for run in range(runs):
        size = total(opens[0:1] & (run_along[0:1] == run), 1)
        size = (size + GROUP - 1) & ~(GROUP - 1)
        base += jnp.where(run_down[:, 0:1] > run, size, 0)
        begins += jnp.where(along[0:1] > side - SCALARS + run, size, 0)
        ahead += size
        unused += jnp.where(along[0:1] >= ahead, span, 0)
    where = base + within + (rank_down >> 1)
    col_at = 2 * slot_bits + 2 * row_bits
    odd = rank_down & 1
    n, row, place = down[:, 0:1], row_down[:, 0:1], place_down[:, 0:1]
    word = jnp.where(odd == 0, n, n << slot_bits)
    word += jnp.where(odd == 0, row, row << row_bits) << (2 * slot_bits)
    word += (jnp.where(odd == 0, place, 0) << col_at) + (1 << (col_at + col_bits))
    word = jnp.broadcast_to(word, shape)
    hit = (where == along) & live_down
    low = total(jnp.where(hit, word & 0xFFFF, 0), 0)
    high = total(jnp.where(hit, word >> 16, 0), 0)
    listed = (high << 16) | low
    unused = jnp.minimum(unused, span * runs - 1) << col_at
    listed = jnp.where(listed == 0, unused, listed)
    words[...] = jnp.where(along[0:1] >= side - SCALARS, begins, listed)


def pair_plan(section, bits, per, span, runs, side, me, counts, rows, cols):
    return pl.pallas_call(
        functools.partial(plan_kernel, section, bits, per, span, runs),
        out_shape=jax.ShapeDtypeStruct((1, side), jnp.int32),
        in_specs=[IN_SMEM, IN_SMEM, IN_VMEM, IN_VMEM],
        out_specs=IN_VMEM,
        scratch_shapes=[pltpu.VMEM((8, side), jnp.int32)],
        compiler_params=pltpu.CompilerParams(vmem_limit_bytes=SMALL_LIMIT),
        cost_estimate=LONG,
    )(me, counts, rows, cols)


def bounds(words, run):
    at = words.shape[-1] - SCALARS + run
    return words[0, at], words[0, at + 1]


def decode_word(word, bits, first_col):
    slot_bits, row_bits, col_bits = bits
    fields = []
    for width in (slot_bits, slot_bits, row_bits, row_bits, col_bits):
        fields.append(word & ((1 << width) - 1))
        word = word >> width
    fields[4] -= first_col
    return (*fields, word)


def fetch_kernel(lump, counts, ratings, out, sem):
    def loads(section):
        def load(i):
            part = pl.ds(i * lump, lump)
            return pltpu.make_async_copy(ratings.at[section, part], out.at[section, part], sem.at[section, i])

        return lax.div(counts[section] + lump - 1, lump), load

    for section in range(ratings.shape[0]):
        lumps, load = loads(section)
        lax.fori_loop(0, lumps, lambda i, c, load=load: (load(i).start(), c)[1], 0)
    for section in range(ratings.shape[0]):
        lumps, load = loads(section)
        lax.fori_loop(0, lumps, lambda i, c, load=load: (load(i).wait(), c)[1], 0)


def fetch(counts, ratings):
    sections, slots = ratings.shape[:2]
    lump = math.gcd(slots, 16)
    return pl.pallas_call(
        functools.partial(fetch_kernel, lump),
        out_shape=jax.ShapeDtypeStruct(ratings.shape, ratings.dtype),
        in_specs=[IN_SMEM, IN_HBM],
        out_specs=IN_VMEM,
        scratch_shapes=[pltpu.SemaphoreType.DMA((sections, slots // lump))],
        compiler_params=pltpu.CompilerParams(vmem_limit_bytes=FETCH_LIMIT),
        cost_estimate=LONG,
    )(counts, ratings)


def gather_tiles(pieces, items):
    at = 0
    for piece in pieces:
        for t in range(piece.shape[0]):
            items[at + t] = piece[t]
        at += piece.shape[0]


def items_kernel(section, run, count, skipped, bits, words, ratings, users, *refs):
    outs, items, grad = refs[count + skipped : -2], refs[-2], refs[-1]
    out_even, *out_odd, misfits = outs
    span = items.shape[0]
    per = span // 2
    tile = users.shape[1]
    low, high = bounds(words, run)
    steps = lax.div(high - low, GROUP)
    gather_tiles(refs[:count], items)
    grad[...] = jnp.zeros_like(grad)

    def decode(p):
        return decode_word(words[0, p], bits, run * span)

    def users_of(row_a, row_b):
        return jnp.concatenate([users[row_a], users[row_b]], axis=0)

    def predict(p):
        slot_a, slot_b, row_a, row_b, col, live = decode(p)
        predicted = lax.dot_general(
            users_of(row_a, row_b), items[col], (((1,), (1,)), ((), ())), preferred_element_type=jnp.float32
        )
        given = jnp.concatenate([ratings[section, slot_a], ratings[section, slot_b]], axis=0).astype(jnp.float32)
        rows = lax.broadcasted_iota(jnp.int32, (2 * tile, 1), 0)
        return jnp.where(rows < tile * live, given - predicted, 0.0).astype(jnp.bfloat16)

    def add_grad(p, misfit):
        _, _, row_a, row_b, col, _ = decode(p)
        grad[col] += lax.dot_general(
            misfit, users_of(row_a, row_b), (((0,), (0,)), ((), ())), preferred_element_type=jnp.float32
        )

    @pl.when(steps > 0)
    def _():
        for j in range(GROUP):
            misfits[j] = predict(low + j)

        def advance(step, carry):
            at = step * GROUP
            held = [misfits[at + j] for j in range(GROUP)]
            following = [predict(low + at + GROUP + j) for j in range(GROUP)]
            for j in range(GROUP):
                add_grad(low + at + j, held[j])
            for j in range(GROUP):
                misfits[at + GROUP + j] = following[j]
            return carry

        lax.fori_loop(0, steps - 1, advance, 0)
        for j in range(GROUP):
            add_grad(high - GROUP + j, misfits[high - low - GROUP + j])

    at = 0
    for out in (out_even, *out_odd):
        for t in range(out.shape[0]):
            out[t] = grad[at + t]
        at += out.shape[0]


def item_grads(section, run, per, bits, words, ratings, users, pieces, after, parts):
    tile, width = users.shape[1:]
    f32 = jnp.float32
    held = per * (users.shape[0] + users.shape[0] % 2)
    held = -(-min(held, ratings.shape[1] // 2 + per) // GROUP) * GROUP
    even_grad, *odd_grads, misfits = pl.pallas_call(
        functools.partial(items_kernel, section, run, len(pieces), len(after), bits),
        out_shape=[jax.ShapeDtypeStruct((per, tile, width), f32)]
        + [jax.ShapeDtypeStruct((per // parts, tile, width), f32)] * parts
        + [jax.ShapeDtypeStruct((held, 2 * tile, tile), jnp.bfloat16)],
        in_specs=[IN_SMEM] + [IN_VMEM] * (2 + len(pieces)) + [ANY] * len(after),
        out_specs=[IN_VMEM] * (2 + parts),
        scratch_shapes=[pltpu.VMEM((2 * per, tile, width), jnp.bfloat16), pltpu.VMEM((2 * per, tile, width), f32)],
        compiler_params=pltpu.CompilerParams(vmem_limit_bytes=SMALL_LIMIT),
        cost_estimate=LONG,
    )(words, ratings, users, *pieces, *after)
    return even_grad, odd_grads, misfits


def add_user_grads(bits, first_run, words, pieces, misfits, items, grad):
    tile = grad.shape[1]
    first_col = first_run * items.shape[0] // len(misfits)
    gather_tiles(pieces, items)
    for run, held in enumerate(misfits, first_run):
        low, high = bounds(words, run)

        def advance(step, carry, low=low, held=held):
            for j in range(GROUP):
                at = step * GROUP + j
                _, _, row_a, row_b, col, _ = decode_word(words[0, low + at], bits, first_col)
                part = jnp.dot(held[at], items[col], preferred_element_type=jnp.float32)
                grad[row_a] += part[:tile]
                grad[row_b] += part[tile:]
            return carry

        lax.fori_loop(0, lax.div(high - low, GROUP), advance, 0)


def users_head_kernel(bits, runs, words, *refs):
    *pieces, grad, items = refs[runs:]
    grad[...] = jnp.zeros_like(grad)
    add_user_grads(bits, 0, words, pieces, refs[:runs], items, grad)


def users_tail_kernel(power, bits, first_run, words, held, *refs):
    *pieces, factors, noise, partial, new, new_bf, items, grad = refs
    grad[...] = partial[...]
    add_user_grads(bits, first_run, words, pieces, [held], items, grad)

    def finish(t, carry):
        before = factors[t]
        after = (
            before + HALF_STEP * (power * grad[t] - PRIOR * before) + ROOT_STEP * noise[t].astype(jnp.float32)
        )
        new[t] = after
        new_bf[t] = after.astype(jnp.bfloat16)
        return carry

    lax.fori_loop(0, factors.shape[0], finish, 0)


def tiles_of(pieces):
    return sum(piece.shape[0] for piece in pieces), *pieces[0].shape[1:]


def users_head(bits, words, misfits, pieces, shape):
    return pl.pallas_call(
        functools.partial(users_head_kernel, bits, len(misfits)),
        out_shape=jax.ShapeDtypeStruct(shape, jnp.float32),
        in_specs=[IN_SMEM] + [IN_VMEM] * (len(misfits) + len(pieces)),
        out_specs=IN_VMEM,
        scratch_shapes=[pltpu.VMEM(tiles_of(pieces), jnp.bfloat16)],
        compiler_params=pltpu.CompilerParams(vmem_limit_bytes=SMALL_LIMIT),
        cost_estimate=BRIEF,
    )(words, *misfits, *pieces)


def users_tail(power, bits, first_run, words, misfits, pieces, factors, noise, partial):
    shape = factors.shape
    return pl.pallas_call(
        functools.partial(users_tail_kernel, power, bits, first_run),
        out_shape=[jax.ShapeDtypeStruct(shape, jnp.float32), jax.ShapeDtypeStruct(shape, jnp.bfloat16)],
        in_specs=[IN_SMEM, IN_VMEM] + [IN_VMEM] * (len(pieces) + 3),
        out_specs=[IN_VMEM] * 2,
        scratch_shapes=[pltpu.VMEM(tiles_of(pieces), jnp.bfloat16), pltpu.VMEM(shape, jnp.float32)],
        compiler_params=pltpu.CompilerParams(vmem_limit_bytes=SMALL_LIMIT),
        cost_estimate=BRIEF,
    )(words, misfits, *pieces, factors, noise, partial)


def coded_shape(per, tile, width):
    return jax.ShapeDtypeStruct((per * tile + SCALE_ROWS, width), jnp.int16)


def encode(blocks, out):
    per = len(blocks)
    tile, width = blocks[0].shape
    row = lax.broadcasted_iota(jnp.int32, (SCALE_ROWS, width), 0)
    powers = jnp.zeros((SCALE_ROWS, width), jnp.int32)
    for t, block in enumerate(blocks):
        largest = jnp.max(jnp.abs(block), axis=0, keepdims=True)
        power = jnp.ceil(SCALE_STEPS * jnp.log2(jnp.maximum(largest, 1e-20)))
        scaled = jnp.round(block * jnp.exp2(15.0 - power / SCALE_STEPS))
        out[pl.ds(t * tile, tile)] = jnp.clip(scaled, -32767.0, 32767.0).astype(jnp.int32).astype(jnp.int16)
        powers = jnp.where(row == t, power.astype(jnp.int32), powers)
    out[pl.ds(per * tile, SCALE_ROWS)] = powers.astype(jnp.int16)


def decoded(ref, t, tile, per):
    powers = ref[pl.ds(per * tile, SCALE_ROWS)].astype(jnp.int32).astype(jnp.float32)
    unit = jnp.exp2(powers[t : t + 1] / SCALE_STEPS - 15.0)
    return ref[pl.ds(t * tile, tile)].astype(jnp.int32).astype(jnp.float32) * unit


def join_kernel(count, mine, *refs):
    others = [ref[t] for ref in refs[:count] for t in range(ref.shape[0])]
    encode([mine[t] + other for t, other in enumerate(others)], refs[-1])


def join(mine, others, after):
    return pl.pallas_call(
        functools.partial(join_kernel, len(others)),
        out_shape=coded_shape(*mine.shape),
        in_specs=[IN_VMEM] * (1 + len(others)) + [ANY] * len(after),
        out_specs=IN_VMEM,
        compiler_params=pltpu.CompilerParams(vmem_limit_bytes=SMALL_LIMIT),
        cost_estimate=BRIEF,
    )(mine, *others, *after)


def owner_sum(mine, other, coded, t):
    per, tile, _ = mine.shape
    total = mine[t] + other[t]
    for ref in coded:
        total = total + decoded(ref, t, tile, per)
    return total


def update_kernel(power, mine, other, *refs):
    *coded, factors, noise, _, new, new_bf = refs
    for t in range(mine.shape[0]):
        step = HALF_STEP * power * owner_sum(mine, other, coded, t) + ROOT_STEP * noise[t].astype(jnp.float32)
        after = factors[t] - HALF_STEP * PRIOR * factors[t] + step
        new[t] = after
        new_bf[t] = after.astype(jnp.bfloat16)


def delta_kernel(power, mine, other, *refs):
    *coded, noise, _, out = refs
    steps = []
    for t in range(mine.shape[0]):
        steps.append(HALF_STEP * power * owner_sum(mine, other, coded, t) + ROOT_STEP * noise[t].astype(jnp.float32))
    encode(steps, out)


def arrive_kernel(coded, factors, new, new_bf):
    per, tile, _ = factors.shape
    for t in range(per):
        after = factors[t] - HALF_STEP * PRIOR * factors[t] + decoded(coded, t, tile, per)
        new[t] = after
        new_bf[t] = after.astype(jnp.bfloat16)


def in_vmem(kernel, out_shape, *operands, after=()):
    return pl.pallas_call(
        kernel,
        out_shape=out_shape,
        in_specs=[IN_VMEM] * len(operands) + [ANY] * len(after),
        out_specs=jax.tree.map(lambda _: IN_VMEM, out_shape),
        compiler_params=pltpu.CompilerParams(vmem_limit_bytes=SMALL_LIMIT),
        cost_estimate=BRIEF,
    )(*operands, *after)


def gathered(own, runs):
    evens = [[own]] + [[swapped(own, "user", 2 * d)] for d in range(1, 3 if runs == 4 else runs)]
    if runs == 4:
        half = own.shape[0] // 2
        evens.append([swapped(evens[1][0][:half], "user", 4), swapped(evens[2][0][half:], "user", 2)])
    return evens


def body(u_factors, v_factors, ratings, tile_rows, tile_cols, tile_counts, u_noise, v_noise):
    tile = ratings.shape[-1]
    sections = ratings.shape[2]
    width = u_factors.shape[1]
    peers = lax.axis_size("user")
    power = float(lax.axis_size("item"))
    me = lax.axis_index("user").astype(jnp.int32).reshape(1)
    users = u_factors.reshape(-1, tile, width)
    items = v_factors.reshape(-1, tile, width)
    per = items.shape[0]
    item_tiles = peers * per
    span = 2 * per
    runs = item_tiles // span
    ratings = ratings.reshape(ratings.shape[2:])
    counts = tile_counts.reshape(sections)
    u_noise = u_noise.reshape(sections, *users.shape)
    v_noise = v_noise.reshape(sections, *items.shape)
    side = -(-ratings.shape[1] // 128) * 128
    assert (ratings.shape[1] + item_tiles) // 2 + runs * GROUP <= side - SCALARS and runs < SCALARS
    assert per & (per - 1) == 0
    bits = widths(ratings.shape[1], users.shape[0], item_tiles)
    pair = (
        jax.ShapeDtypeStruct(items.shape, jnp.float32),
        jax.ShapeDtypeStruct(items.shape, jnp.bfloat16),
    )
    rated = fetch(counts, ratings)
    items_bf = items.astype(jnp.bfloat16)
    users_bf = users.astype(jnp.bfloat16)
    for section in range(sections):
        sent = shifted(items_bf, "item", section) if section else items_bf
        evens = gathered(sent, runs)
        chunks = [even + [swapped(piece, "user", 1) for piece in even] for even in evens]
        words = pair_plan(section, bits, per, span, runs, side, me, counts, tile_rows, tile_cols)
        mine, other, sums, misfits = [], [], [], []
        after = []
        for run in range(runs):
            if run in (1, 2):
                after += evens[run + 1]
            even_grad, odd_grads, held = item_grads(
                section, run, per, bits, words, rated, users_bf, chunks[run], after, 2 if run else 1
            )
            misfits.append(held)
            mine.append(even_grad)
            other.append([swapped(grad, "user", 1) for grad in odd_grads])
            after = [even_grad]
            if run >= 2:
                coded = join(mine[run - 1], other[run - 1], after)
                sums.append(swapped(coded, "user", 2 * (run - 1)))
                after = [coded]
        coded = join(mine[-1], other[-1], after + sums[:1])
        sums.append(swapped(coded, "user", 2 * (runs - 1)))
        head = [piece for chunk in chunks[:-1] for piece in chunk]
        partial = users_head(bits, words, misfits[:-1], head, users.shape)
        if section == 0:
            items, items_bf = in_vmem(
                functools.partial(update_kernel, power),
                pair,
                mine[0],
                other[0][0],
                *sums,
                items,
                v_noise[section],
                after=(partial,),
            )
        else:
            delta = in_vmem(
                functools.partial(delta_kernel, power),
                coded_shape(*items.shape),
                mine[0],
                other[0][0],
                *sums,
                v_noise[section],
                after=(partial,),
            )
            items, items_bf = in_vmem(arrive_kernel, pair, shifted(delta, "item", -section), items)
        users, users_bf = users_tail(
            power, bits, runs - 1, words, misfits[-1], chunks[-1], users, u_noise[section], partial
        )
    return (users.reshape(u_factors.shape), items.reshape(v_factors.shape))


def solution(mesh):
    placed = (
        P(("user", "item"), None),
        P(("item", "user"), None),
        P("user", "item", None, None, None, None),
        P("user", "item", None, None),
        P("user", "item", None, None),
        P("user", "item", None),
        P(None, ("user", "item"), None),
        P(None, ("item", "user"), None),
    )
    return jax.shard_map(
        body,
        mesh=mesh,
        in_specs=placed,
        out_specs=(P(("user", "item"), None), P(("item", "user"), None)),
        check_vma=False,
    )
```

```python
import functools
import math

import jax
import jax.numpy as jnp
from jax import lax
from jax.experimental import pallas as pl
from jax.experimental.pallas import tpu as pltpu
from jax.sharding import PartitionSpec as P

HALF_STEP = 0.002
ROOT_STEP = math.sqrt(0.004)
PRIOR = 25.0
GROUP = 4
SCALE_ROWS = 16
SMALL_LIMIT = 12 * 2**20
FETCH_LIMIT = 38 * 2**20
SCALE_STEPS = 128.0
SCALARS = 16
LONG = pl.CostEstimate(flops=4 * 10**9, bytes_accessed=2**12, transcendentals=0)
BRIEF = pl.CostEstimate(flops=10**8, bytes_accessed=2**12, transcendentals=0)

ANY = pl.BlockSpec(memory_space=pl.ANY)
IN_HBM = pl.BlockSpec(memory_space=pltpu.HBM)
IN_VMEM = pl.BlockSpec(memory_space=pltpu.VMEM)
IN_SMEM = pl.BlockSpec(memory_space=pltpu.SMEM)


def shifted(x, axis, by):
    peers = lax.axis_size(axis)
    return lax.ppermute(x, axis, [(i, (i + by) % peers) for i in range(peers)])


def swapped(x, axis, mask):
    peers = lax.axis_size(axis)
    return lax.ppermute(x, axis, [(i, i ^ mask) for i in range(peers)])


def widths(slots, user_tiles, item_tiles):
    bits = tuple(max(1, (n - 1).bit_length()) for n in (slots, user_tiles, item_tiles))
    assert 2 * bits[0] + 2 * bits[1] + bits[2] + 2 <= 31
    return bits


def total(x, axis):
    return jnp.sum(x.astype(jnp.float32), axis=axis, keepdims=True).astype(jnp.int32)


def plan_kernel(section, bits, per, span, runs, me, counts, rows, cols, words, lists):
    slot_bits, row_bits, col_bits = bits
    side = lists.shape[-1]
    slots = rows.shape[-1]
    shape = (side, side)
    count = counts[section]
    lists[...] = jnp.zeros_like(lists)
    lists[0:1, 0:slots] = rows[0, 0, section : section + 1]
    lists[1:2, 0:slots] = cols[0, 0, section : section + 1]
    along = lax.broadcasted_iota(jnp.int32, shape, 1)
    down = lax.broadcasted_iota(jnp.int32, shape, 0)
    row_along = jnp.broadcast_to(lists[0:1], shape)
    place_along = jnp.broadcast_to(lists[1:2] ^ (me[0] * per), shape)
    key = (place_along << row_bits | row_along).astype(jnp.float32).T.astype(jnp.int32)
    row_down = key & ((1 << row_bits) - 1)
    place_down = key >> row_bits
    span_bits = span.bit_length() - 1
    run_along, run_down = place_along >> span_bits, place_down >> span_bits
    live_along, live_down = along < count, down < count
    same = place_along == place_down
    rank_down = total(same & live_along & (row_along < row_down), 1)
    rank_along = total(same & live_down & (row_down < row_along), 0)
    opens = live_along & ((rank_along & 1) == 0)
    within = total(opens & (run_along == run_down) & (place_along < place_down), 1)
    base = jnp.zeros((side, 1), jnp.int32)
    begins = jnp.zeros((1, side), jnp.int32)
    unused = jnp.zeros((1, side), jnp.int32)
    ahead = jnp.zeros((1, 1), jnp.int32)
    for run in range(runs):
        size = total(opens[0:1] & (run_along[0:1] == run), 1)
        size = (size + GROUP - 1) & ~(GROUP - 1)
        base += jnp.where(run_down[:, 0:1] > run, size, 0)
        begins += jnp.where(along[0:1] > side - SCALARS + run, size, 0)
        ahead += size
        unused += jnp.where(along[0:1] >= ahead, span, 0)
    where = base + within + (rank_down >> 1)
    col_at = 2 * slot_bits + 2 * row_bits
    odd = rank_down & 1
    n, row, place = down[:, 0:1], row_down[:, 0:1], place_down[:, 0:1]
    word = jnp.where(odd == 0, n, n << slot_bits)
    word += jnp.where(odd == 0, row, row << row_bits) << (2 * slot_bits)
    word += (jnp.where(odd == 0, place, 0) << col_at) + (1 << (col_at + col_bits))
    word = jnp.broadcast_to(word, shape)
    hit = (where == along) & live_down
    low = total(jnp.where(hit, word & 0xFFFF, 0), 0)
    high = total(jnp.where(hit, word >> 16, 0), 0)
    listed = (high << 16) | low
    unused = jnp.minimum(unused, span * runs - 1) << col_at
    listed = jnp.where(listed == 0, unused, listed)
    words[...] = jnp.where(along[0:1] >= side - SCALARS, begins, listed)


def pair_plan(section, bits, per, span, runs, side, me, counts, rows, cols):
    return pl.pallas_call(
        functools.partial(plan_kernel, section, bits, per, span, runs),
        out_shape=jax.ShapeDtypeStruct((1, side), jnp.int32),
        in_specs=[IN_SMEM, IN_SMEM, IN_VMEM, IN_VMEM],
        out_specs=IN_VMEM,
        scratch_shapes=[pltpu.VMEM((8, side), jnp.int32)],
        compiler_params=pltpu.CompilerParams(vmem_limit_bytes=SMALL_LIMIT),
        cost_estimate=LONG,
    )(me, counts, rows, cols)


def bounds(words, run):
    at = words.shape[-1] - SCALARS + run
    return words[0, at], words[0, at + 1]


def decode_word(word, bits, first_col):
    slot_bits, row_bits, col_bits = bits
    fields = []
    for width in (slot_bits, slot_bits, row_bits, row_bits, col_bits):
        fields.append(word & ((1 << width) - 1))
        word = word >> width
    fields[4] -= first_col
    return (*fields, word)


def fetch_kernel(lump, counts, ratings, out, sem):
    def loads(section):
        def load(i):
            part = pl.ds(i * lump, lump)
            return pltpu.make_async_copy(ratings.at[section, part], out.at[section, part], sem.at[section, i])

        return lax.div(counts[section] + lump - 1, lump), load

    for section in range(ratings.shape[0]):
        lumps, load = loads(section)
        lax.fori_loop(0, lumps, lambda i, c, load=load: (load(i).start(), c)[1], 0)
    for section in range(ratings.shape[0]):
        lumps, load = loads(section)
        lax.fori_loop(0, lumps, lambda i, c, load=load: (load(i).wait(), c)[1], 0)


def fetch(counts, ratings):
    sections, slots = ratings.shape[:2]
    lump = math.gcd(slots, 16)
    return pl.pallas_call(
        functools.partial(fetch_kernel, lump),
        out_shape=jax.ShapeDtypeStruct(ratings.shape, ratings.dtype),
        in_specs=[IN_SMEM, IN_HBM],
        out_specs=IN_VMEM,
        scratch_shapes=[pltpu.SemaphoreType.DMA((sections, slots // lump))],
        compiler_params=pltpu.CompilerParams(vmem_limit_bytes=FETCH_LIMIT),
        cost_estimate=LONG,
    )(counts, ratings)


def gather_tiles(pieces, items):
    at = 0
    for piece in pieces:
        for t in range(piece.shape[0]):
            items[at + t] = piece[t]
        at += piece.shape[0]


def items_kernel(section, run, count, skipped, bits, words, ratings, users, *refs):
    outs, items, grad = refs[count + skipped : -2], refs[-2], refs[-1]
    out_even, *out_odd, misfits = outs
    span = items.shape[0]
    per = span // 2
    tile = users.shape[1]
    low, high = bounds(words, run)
    steps = lax.div(high - low, GROUP)
    gather_tiles(refs[:count], items)
    grad[...] = jnp.zeros_like(grad)

    def decode(p):
        return decode_word(words[0, p], bits, run * span)

    def users_of(row_a, row_b):
        return jnp.concatenate([users[row_a], users[row_b]], axis=0)

    def predict(p):
        slot_a, slot_b, row_a, row_b, col, live = decode(p)
        predicted = lax.dot_general(
            users_of(row_a, row_b), items[col], (((1,), (1,)), ((), ())), preferred_element_type=jnp.float32
        )
        given = jnp.concatenate([ratings[section, slot_a], ratings[section, slot_b]], axis=0).astype(jnp.float32)
        rows = lax.broadcasted_iota(jnp.int32, (2 * tile, 1), 0)
        return jnp.where(rows < tile * live, given - predicted, 0.0).astype(jnp.bfloat16)

    def add_grad(p, misfit):
        _, _, row_a, row_b, col, _ = decode(p)
        grad[col] += lax.dot_general(
            misfit, users_of(row_a, row_b), (((0,), (0,)), ((), ())), preferred_element_type=jnp.float32
        )

    @pl.when(steps > 0)
    def _():
        for j in range(GROUP):
            misfits[j] = predict(low + j)

        def advance(step, carry):
            at = step * GROUP
            held = [misfits[at + j] for j in range(GROUP)]
            following = [predict(low + at + GROUP + j) for j in range(GROUP)]
            for j in range(GROUP):
                add_grad(low + at + j, held[j])
            for j in range(GROUP):
                misfits[at + GROUP + j] = following[j]
            return carry

        lax.fori_loop(0, steps - 1, advance, 0)
        for j in range(GROUP):
            add_grad(high - GROUP + j, misfits[high - low - GROUP + j])

    at = 0
    for out in (out_even, *out_odd):
        for t in range(out.shape[0]):
            out[t] = grad[at + t]
        at += out.shape[0]


def item_grads(section, run, per, bits, words, ratings, users, pieces, after, parts):
    tile, width = users.shape[1:]
    f32 = jnp.float32
    held = per * (users.shape[0] + users.shape[0] % 2)
    held = -(-min(held, ratings.shape[1] // 2 + per) // GROUP) * GROUP
    even_grad, *odd_grads, misfits = pl.pallas_call(
        functools.partial(items_kernel, section, run, len(pieces), len(after), bits),
        out_shape=[jax.ShapeDtypeStruct((per, tile, width), f32)]
        + [jax.ShapeDtypeStruct((per // parts, tile, width), f32)] * parts
        + [jax.ShapeDtypeStruct((held, 2 * tile, tile), jnp.bfloat16)],
        in_specs=[IN_SMEM] + [IN_VMEM] * (2 + len(pieces)) + [ANY] * len(after),
        out_specs=[IN_VMEM] * (2 + parts),
        scratch_shapes=[pltpu.VMEM((2 * per, tile, width), jnp.bfloat16), pltpu.VMEM((2 * per, tile, width), f32)],
        compiler_params=pltpu.CompilerParams(vmem_limit_bytes=SMALL_LIMIT),
        cost_estimate=LONG,
    )(words, ratings, users, *pieces, *after)
    return even_grad, odd_grads, misfits


def add_user_grads(bits, first_run, words, pieces, misfits, items, grad):
    tile = grad.shape[1]
    first_col = first_run * items.shape[0] // len(misfits)
    gather_tiles(pieces, items)
    for run, held in enumerate(misfits, first_run):
        low, high = bounds(words, run)

        def advance(step, carry, low=low, held=held):
            for j in range(GROUP):
                at = step * GROUP + j
                _, _, row_a, row_b, col, _ = decode_word(words[0, low + at], bits, first_col)
                part = jnp.dot(held[at], items[col], preferred_element_type=jnp.float32)
                grad[row_a] += part[:tile]
                grad[row_b] += part[tile:]
            return carry

        lax.fori_loop(0, lax.div(high - low, GROUP), advance, 0)


def users_head_kernel(bits, runs, words, *refs):
    *pieces, grad, items = refs[runs:]
    grad[...] = jnp.zeros_like(grad)
    add_user_grads(bits, 0, words, pieces, refs[:runs], items, grad)


def users_tail_kernel(power, bits, first_run, words, held, *refs):
    *pieces, factors, noise, partial, new, new_bf, items, grad = refs
    grad[...] = partial[...]
    add_user_grads(bits, first_run, words, pieces, [held], items, grad)

    def finish(t, carry):
        before = factors[t]
        after = (
            before + HALF_STEP * (power * grad[t] - PRIOR * before) + ROOT_STEP * noise[t].astype(jnp.float32)
        )
        new[t] = after
        new_bf[t] = after.astype(jnp.bfloat16)
        return carry

    lax.fori_loop(0, factors.shape[0], finish, 0)


def tiles_of(pieces):
    return sum(piece.shape[0] for piece in pieces), *pieces[0].shape[1:]


def users_head(bits, words, misfits, pieces, shape):
    return pl.pallas_call(
        functools.partial(users_head_kernel, bits, len(misfits)),
        out_shape=jax.ShapeDtypeStruct(shape, jnp.float32),
        in_specs=[IN_SMEM] + [IN_VMEM] * (len(misfits) + len(pieces)),
        out_specs=IN_VMEM,
        scratch_shapes=[pltpu.VMEM(tiles_of(pieces), jnp.bfloat16)],
        compiler_params=pltpu.CompilerParams(vmem_limit_bytes=SMALL_LIMIT),
        cost_estimate=BRIEF,
    )(words, *misfits, *pieces)


def users_tail(power, bits, first_run, words, misfits, pieces, factors, noise, partial):
    shape = factors.shape
    return pl.pallas_call(
        functools.partial(users_tail_kernel, power, bits, first_run),
        out_shape=[jax.ShapeDtypeStruct(shape, jnp.float32), jax.ShapeDtypeStruct(shape, jnp.bfloat16)],
        in_specs=[IN_SMEM, IN_VMEM] + [IN_VMEM] * (len(pieces) + 3),
        out_specs=[IN_VMEM] * 2,
        scratch_shapes=[pltpu.VMEM(tiles_of(pieces), jnp.bfloat16), pltpu.VMEM(shape, jnp.float32)],
        compiler_params=pltpu.CompilerParams(vmem_limit_bytes=SMALL_LIMIT),
        cost_estimate=BRIEF,
    )(words, misfits, *pieces, factors, noise, partial)


def coded_shape(per, tile, width):
    return jax.ShapeDtypeStruct((per * tile + SCALE_ROWS, width), jnp.int16)


def encode(blocks, out):
    per = len(blocks)
    tile, width = blocks[0].shape
    row = lax.broadcasted_iota(jnp.int32, (SCALE_ROWS, width), 0)
    powers = jnp.zeros((SCALE_ROWS, width), jnp.int32)
    for t, block in enumerate(blocks):
        largest = jnp.max(jnp.abs(block), axis=0, keepdims=True)
        power = jnp.ceil(SCALE_STEPS * jnp.log2(jnp.maximum(largest, 1e-20)))
        scaled = jnp.round(block * jnp.exp2(15.0 - power / SCALE_STEPS))
        out[pl.ds(t * tile, tile)] = jnp.clip(scaled, -32767.0, 32767.0).astype(jnp.int32).astype(jnp.int16)
        powers = jnp.where(row == t, power.astype(jnp.int32), powers)
    out[pl.ds(per * tile, SCALE_ROWS)] = powers.astype(jnp.int16)


def decoded(ref, t, tile, per):
    powers = ref[pl.ds(per * tile, SCALE_ROWS)].astype(jnp.int32).astype(jnp.float32)
    unit = jnp.exp2(powers[t : t + 1] / SCALE_STEPS - 15.0)
    return ref[pl.ds(t * tile, tile)].astype(jnp.int32).astype(jnp.float32) * unit


def join_kernel(count, mine, *refs):
    others = [ref[t] for ref in refs[:count] for t in range(ref.shape[0])]
    encode([mine[t] + other for t, other in enumerate(others)], refs[-1])


def join(mine, others, after):
    return pl.pallas_call(
        functools.partial(join_kernel, len(others)),
        out_shape=coded_shape(*mine.shape),
        in_specs=[IN_VMEM] * (1 + len(others)) + [ANY] * len(after),
        out_specs=IN_VMEM,
        compiler_params=pltpu.CompilerParams(vmem_limit_bytes=SMALL_LIMIT),
        cost_estimate=BRIEF,
    )(mine, *others, *after)


def owner_sum(mine, other, coded, t):
    per, tile, _ = mine.shape
    total = mine[t] + other[t]
    for ref in coded:
        total = total + decoded(ref, t, tile, per)
    return total


def update_kernel(power, mine, other, *refs):
    *coded, factors, noise, _, new, new_bf = refs
    for t in range(mine.shape[0]):
        step = HALF_STEP * power * owner_sum(mine, other, coded, t) + ROOT_STEP * noise[t].astype(jnp.float32)
        after = factors[t] - HALF_STEP * PRIOR * factors[t] + step
        new[t] = after
        new_bf[t] = after.astype(jnp.bfloat16)


def delta_kernel(power, mine, other, *refs):
    *coded, noise, _, out = refs
    steps = []
    for t in range(mine.shape[0]):
        steps.append(HALF_STEP * power * owner_sum(mine, other, coded, t) + ROOT_STEP * noise[t].astype(jnp.float32))
    encode(steps, out)


def arrive_kernel(coded, factors, new, new_bf):
    per, tile, _ = factors.shape
    for t in range(per):
        after = factors[t] - HALF_STEP * PRIOR * factors[t] + decoded(coded, t, tile, per)
        new[t] = after
        new_bf[t] = after.astype(jnp.bfloat16)


def pass_kernel(given, *refs):
    refs[-1][...] = given[...]


def in_vmem(kernel, out_shape, *operands, after=()):
    return pl.pallas_call(
        kernel,
        out_shape=out_shape,
        in_specs=[IN_VMEM] * len(operands) + [ANY] * len(after),
        out_specs=jax.tree.map(lambda _: IN_VMEM, out_shape),
        compiler_params=pltpu.CompilerParams(vmem_limit_bytes=SMALL_LIMIT),
        cost_estimate=BRIEF,
    )(*operands, *after)


def gathered(own, runs):
    evens = [own]
    for d in range(1, runs):
        relayed = runs == 4 and d == 3
        evens.append(swapped(evens[1] if relayed else own, "user", 4 if relayed else 2 * d))
    return evens


def body(u_factors, v_factors, ratings, tile_rows, tile_cols, tile_counts, u_noise, v_noise):
    tile = ratings.shape[-1]
    sections = ratings.shape[2]
    width = u_factors.shape[1]
    peers = lax.axis_size("user")
    power = float(lax.axis_size("item"))
    me = lax.axis_index("user").astype(jnp.int32).reshape(1)
    users = u_factors.reshape(-1, tile, width)
    items = v_factors.reshape(-1, tile, width)
    per = items.shape[0]
    item_tiles = peers * per
    span = 2 * per
    runs = item_tiles // span
    ratings = ratings.reshape(ratings.shape[2:])
    counts = tile_counts.reshape(sections)
    u_noise = u_noise.reshape(sections, *users.shape)
    v_noise = v_noise.reshape(sections, *items.shape)
    side = -(-ratings.shape[1] // 128) * 128
    assert (ratings.shape[1] + item_tiles) // 2 + runs * GROUP <= side - SCALARS and runs < SCALARS
    assert per & (per - 1) == 0
    bits = widths(ratings.shape[1], users.shape[0], item_tiles)
    pair = (
        jax.ShapeDtypeStruct(items.shape, jnp.float32),
        jax.ShapeDtypeStruct(items.shape, jnp.bfloat16),
    )
    rated = fetch(counts, ratings)
    items_bf = items.astype(jnp.bfloat16)
    users_bf = users.astype(jnp.bfloat16)
    for section in range(sections):
        words = pair_plan(section, bits, per, span, runs, side, me, counts, tile_rows, tile_cols)
        sent = items_bf
        if section:
            sent = shifted(items_bf, "item", section)
            sent = in_vmem(pass_kernel, jax.ShapeDtypeStruct(sent.shape, sent.dtype), sent, after=(users_bf, words))
        evens = gathered(sent, runs)
        chunks = [[even, swapped(even, "user", 1)] for even in evens]
        mine, other, sums, misfits = {}, {}, {}, {}
        after = [evens[2]]
        order = [(item_grads, run) for run in range(1, runs - 1)]
        order += [(join, run) for run in range(1, runs - 1)]
        order += [(item_grads, 0), (item_grads, runs - 1), (join, runs - 1)]
        for call, run in order:
            if call is item_grads:
                mine[run], odd_grads, misfits[run] = item_grads(
                    section, run, per, bits, words, rated, users_bf, chunks[run], after, 2 if run else 1
                )
                other[run] = [swapped(grad, "user", 1) for grad in odd_grads]
                after = [mine[run]]
            else:
                if run == runs - 1:
                    after += list(sums.values())
                after = [join(mine[run], other[run], after)]
                sums[run] = swapped(after[0], "user", 2 * run)
        sums = [sums[run] for run in range(1, runs)]
        misfits = [misfits[run] for run in range(runs)]
        head = [piece for chunk in chunks[:-1] for piece in chunk]
        partial = users_head(bits, words, misfits[:-1], head, users.shape)
        if section == 0:
            items, items_bf = in_vmem(
                functools.partial(update_kernel, power),
                pair,
                mine[0],
                other[0][0],
                *sums,
                items,
                v_noise[section],
                after=(partial,),
            )
        else:
            delta = in_vmem(
                functools.partial(delta_kernel, power),
                coded_shape(*items.shape),
                mine[0],
                other[0][0],
                *sums,
                v_noise[section],
                after=(partial,),
            )
            items, items_bf = in_vmem(arrive_kernel, pair, shifted(delta, "item", -section), items)
        users, users_bf = users_tail(
            power, bits, runs - 1, words, misfits[-1], chunks[-1], users, u_noise[section], partial
        )
    return (users.reshape(u_factors.shape), items.reshape(v_factors.shape))


def solution(mesh):
    placed = (
        P(("user", "item"), None),
        P(("item", "user"), None),
        P("user", "item", None, None, None, None),
        P("user", "item", None, None),
        P("user", "item", None, None),
        P("user", "item", None),
        P(None, ("user", "item"), None),
        P(None, ("item", "user"), None),
    )
    return jax.shard_map(
        body,
        mesh=mesh,
        in_specs=placed,
        out_specs=(P(("user", "item"), None), P(("item", "user"), None)),
        check_vma=False,
    )
```

```python
import functools
import math

import jax
import jax.numpy as jnp
from jax import lax
from jax.experimental import pallas as pl
from jax.experimental.pallas import tpu as pltpu
from jax.sharding import PartitionSpec as P

HALF_STEP = 0.002
ROOT_STEP = math.sqrt(0.004)
PRIOR = 25.0
GROUP = 4
SCALE_ROWS = 16
SMALL_LIMIT = 12 * 2**20
FETCH_LIMIT = 38 * 2**20
SCALE_STEPS = 128.0
SCALARS = 16
LONG = pl.CostEstimate(flops=4 * 10**9, bytes_accessed=2**12, transcendentals=0)
BRIEF = pl.CostEstimate(flops=10**8, bytes_accessed=2**12, transcendentals=0)

ANY = pl.BlockSpec(memory_space=pl.ANY)
IN_HBM = pl.BlockSpec(memory_space=pltpu.HBM)
IN_VMEM = pl.BlockSpec(memory_space=pltpu.VMEM)
IN_SMEM = pl.BlockSpec(memory_space=pltpu.SMEM)


def shifted(x, axis, by):
    peers = lax.axis_size(axis)
    return lax.ppermute(x, axis, [(i, (i + by) % peers) for i in range(peers)])


def swapped(x, axis, mask):
    peers = lax.axis_size(axis)
    return lax.ppermute(x, axis, [(i, i ^ mask) for i in range(peers)])


def widths(slots, user_tiles, item_tiles):
    bits = tuple(max(1, (n - 1).bit_length()) for n in (slots, user_tiles, item_tiles))
    assert 2 * bits[0] + 2 * bits[1] + bits[2] + 2 <= 31
    return bits


def total(x, axis):
    return jnp.sum(x.astype(jnp.float32), axis=axis, keepdims=True).astype(jnp.int32)


def plan_kernel(section, bits, per, span, runs, me, counts, rows, cols, words, lists):
    slot_bits, row_bits, col_bits = bits
    side = lists.shape[-1]
    slots = rows.shape[-1]
    shape = (side, side)
    count = counts[section]
    lists[...] = jnp.zeros_like(lists)
    lists[0:1, 0:slots] = rows[0, 0, section : section + 1]
    lists[1:2, 0:slots] = cols[0, 0, section : section + 1]
    along = lax.broadcasted_iota(jnp.int32, shape, 1)
    down = lax.broadcasted_iota(jnp.int32, shape, 0)
    row_along = jnp.broadcast_to(lists[0:1], shape)
    place_along = jnp.broadcast_to(lists[1:2] ^ (me[0] * per), shape)
    key = (place_along << row_bits | row_along).astype(jnp.float32).T.astype(jnp.int32)
    row_down = key & ((1 << row_bits) - 1)
    place_down = key >> row_bits
    span_bits = span.bit_length() - 1
    run_along, run_down = place_along >> span_bits, place_down >> span_bits
    live_along, live_down = along < count, down < count
    same = place_along == place_down
    rank_down = total(same & live_along & (row_along < row_down), 1)
    rank_along = total(same & live_down & (row_down < row_along), 0)
    opens = live_along & ((rank_along & 1) == 0)
    within = total(opens & (run_along == run_down) & (place_along < place_down), 1)
    base = jnp.zeros((side, 1), jnp.int32)
    begins = jnp.zeros((1, side), jnp.int32)
    unused = jnp.zeros((1, side), jnp.int32)
    ahead = jnp.zeros((1, 1), jnp.int32)
    for run in range(runs):
        size = total(opens[0:1] & (run_along[0:1] == run), 1)
        size = (size + GROUP - 1) & ~(GROUP - 1)
        base += jnp.where(run_down[:, 0:1] > run, size, 0)
        begins += jnp.where(along[0:1] > side - SCALARS + run, size, 0)
        ahead += size
        unused += jnp.where(along[0:1] >= ahead, span, 0)
    where = base + within + (rank_down >> 1)
    col_at = 2 * slot_bits + 2 * row_bits
    odd = rank_down & 1
    n, row, place = down[:, 0:1], row_down[:, 0:1], place_down[:, 0:1]
    word = jnp.where(odd == 0, n, n << slot_bits)
    word += jnp.where(odd == 0, row, row << row_bits) << (2 * slot_bits)
    word += (jnp.where(odd == 0, place, 0) << col_at) + (1 << (col_at + col_bits))
    word = jnp.broadcast_to(word, shape)
    hit = (where == along) & live_down
    low = total(jnp.where(hit, word & 0xFFFF, 0), 0)
    high = total(jnp.where(hit, word >> 16, 0), 0)
    listed = (high << 16) | low
    unused = jnp.minimum(unused, span * runs - 1) << col_at
    listed = jnp.where(listed == 0, unused, listed)
    words[...] = jnp.where(along[0:1] >= side - SCALARS, begins, listed)


def pair_plan(section, bits, per, span, runs, side, me, counts, rows, cols):
    return pl.pallas_call(
        functools.partial(plan_kernel, section, bits, per, span, runs),
        out_shape=jax.ShapeDtypeStruct((1, side), jnp.int32),
        in_specs=[IN_SMEM, IN_SMEM, IN_VMEM, IN_VMEM],
        out_specs=IN_VMEM,
        scratch_shapes=[pltpu.VMEM((8, side), jnp.int32)],
        compiler_params=pltpu.CompilerParams(vmem_limit_bytes=SMALL_LIMIT),
        cost_estimate=LONG,
    )(me, counts, rows, cols)


def bounds(words, run):
    at = words.shape[-1] - SCALARS + run
    return words[0, at], words[0, at + 1]


def decode_word(word, bits, first_col):
    slot_bits, row_bits, col_bits = bits
    fields = []
    for width in (slot_bits, slot_bits, row_bits, row_bits, col_bits):
        fields.append(word & ((1 << width) - 1))
        word = word >> width
    fields[4] -= first_col
    return (*fields, word)


def fetch_kernel(lump, counts, ratings, out, sem):
    def loads(section):
        def load(i):
            part = pl.ds(i * lump, lump)
            return pltpu.make_async_copy(ratings.at[section, part], out.at[section, part], sem.at[section, i])

        return lax.div(counts[section] + lump - 1, lump), load

    for section in range(ratings.shape[0]):
        lumps, load = loads(section)
        lax.fori_loop(0, lumps, lambda i, c, load=load: (load(i).start(), c)[1], 0)
    for section in range(ratings.shape[0]):
        lumps, load = loads(section)
        lax.fori_loop(0, lumps, lambda i, c, load=load: (load(i).wait(), c)[1], 0)


def fetch(counts, ratings):
    sections, slots = ratings.shape[:2]
    lump = math.gcd(slots, 16)
    return pl.pallas_call(
        functools.partial(fetch_kernel, lump),
        out_shape=jax.ShapeDtypeStruct(ratings.shape, ratings.dtype),
        in_specs=[IN_SMEM, IN_HBM],
        out_specs=IN_VMEM,
        scratch_shapes=[pltpu.SemaphoreType.DMA((sections, slots // lump))],
        compiler_params=pltpu.CompilerParams(vmem_limit_bytes=FETCH_LIMIT),
        cost_estimate=LONG,
    )(counts, ratings)


def gather_tiles(pieces, items):
    at = 0
    for piece in pieces:
        for t in range(piece.shape[0]):
            items[at + t] = piece[t]
        at += piece.shape[0]


def items_kernel(section, run, count, skipped, bits, words, ratings, users, *refs):
    outs, items, grad = refs[count + skipped : -2], refs[-2], refs[-1]
    out_even, *out_odd, misfits = outs
    span = items.shape[0]
    per = span // 2
    tile = users.shape[1]
    low, high = bounds(words, run)
    steps = lax.div(high - low, GROUP)
    gather_tiles(refs[:count], items)
    grad[...] = jnp.zeros_like(grad)

    def decode(p):
        return decode_word(words[0, p], bits, run * span)

    def users_of(row_a, row_b):
        return jnp.concatenate([users[row_a], users[row_b]], axis=0)

    def predict(p):
        slot_a, slot_b, row_a, row_b, col, live = decode(p)
        predicted = lax.dot_general(
            users_of(row_a, row_b), items[col], (((1,), (1,)), ((), ())), preferred_element_type=jnp.float32
        )
        given = jnp.concatenate([ratings[section, slot_a], ratings[section, slot_b]], axis=0).astype(jnp.float32)
        rows = lax.broadcasted_iota(jnp.int32, (2 * tile, 1), 0)
        return jnp.where(rows < tile * live, given - predicted, 0.0).astype(jnp.bfloat16)

    def add_grad(p, misfit):
        _, _, row_a, row_b, col, _ = decode(p)
        grad[col] += lax.dot_general(
            misfit, users_of(row_a, row_b), (((0,), (0,)), ((), ())), preferred_element_type=jnp.float32
        )

    @pl.when(steps > 0)
    def _():
        for j in range(GROUP):
            misfits[j] = predict(low + j)

        def advance(step, carry):
            at = step * GROUP
            held = [misfits[at + j] for j in range(GROUP)]
            following = [predict(low + at + GROUP + j) for j in range(GROUP)]
            for j in range(GROUP):
                add_grad(low + at + j, held[j])
            for j in range(GROUP):
                misfits[at + GROUP + j] = following[j]
            return carry

        lax.fori_loop(0, steps - 1, advance, 0)
        for j in range(GROUP):
            add_grad(high - GROUP + j, misfits[high - low - GROUP + j])

    at = 0
    for out in (out_even, *out_odd):
        for t in range(out.shape[0]):
            out[t] = grad[at + t]
        at += out.shape[0]


def item_grads(section, run, per, bits, words, ratings, users, pieces, after, parts):
    tile, width = users.shape[1:]
    f32 = jnp.float32
    held = per * (users.shape[0] + users.shape[0] % 2)
    held = -(-min(held, ratings.shape[1] // 2 + per) // GROUP) * GROUP
    even_grad, *odd_grads, misfits = pl.pallas_call(
        functools.partial(items_kernel, section, run, len(pieces), len(after), bits),
        out_shape=[jax.ShapeDtypeStruct((per, tile, width), f32)]
        + [jax.ShapeDtypeStruct((per // parts, tile, width), f32)] * parts
        + [jax.ShapeDtypeStruct((held, 2 * tile, tile), jnp.bfloat16)],
        in_specs=[IN_SMEM] + [IN_VMEM] * (2 + len(pieces)) + [ANY] * len(after),
        out_specs=[IN_VMEM] * (2 + parts),
        scratch_shapes=[pltpu.VMEM((2 * per, tile, width), jnp.bfloat16), pltpu.VMEM((2 * per, tile, width), f32)],
        compiler_params=pltpu.CompilerParams(vmem_limit_bytes=SMALL_LIMIT),
        cost_estimate=LONG,
    )(words, ratings, users, *pieces, *after)
    return even_grad, odd_grads, misfits


def add_user_grads(bits, words, pieces, misfits, items, grad):
    tile = grad.shape[1]
    gather_tiles(pieces, items)
    for run, held in enumerate(misfits):
        low, high = bounds(words, run)

        def advance(step, carry, low=low, held=held):
            for j in range(GROUP):
                at = step * GROUP + j
                _, _, row_a, row_b, col, _ = decode_word(words[0, low + at], bits, 0)
                part = jnp.dot(held[at], items[col], preferred_element_type=jnp.float32)
                grad[row_a] += part[:tile]
                grad[row_b] += part[tile:]
            return carry

        lax.fori_loop(0, lax.div(high - low, GROUP), advance, 0)


def users_kernel(power, bits, runs, words, *refs):
    *pieces, factors, noise, new, new_bf, items, grad = refs[runs:]
    grad[...] = jnp.zeros_like(grad)
    add_user_grads(bits, words, pieces, refs[:runs], items, grad)

    def finish(t, carry):
        before = factors[t]
        after = (
            before + HALF_STEP * (power * grad[t] - PRIOR * before) + ROOT_STEP * noise[t].astype(jnp.float32)
        )
        new[t] = after
        new_bf[t] = after.astype(jnp.bfloat16)
        return carry

    lax.fori_loop(0, factors.shape[0], finish, 0)


def tiles_of(pieces):
    return sum(piece.shape[0] for piece in pieces), *pieces[0].shape[1:]


def user_step(power, bits, words, misfits, pieces, factors, noise):
    shape = factors.shape
    return pl.pallas_call(
        functools.partial(users_kernel, power, bits, len(misfits)),
        out_shape=[jax.ShapeDtypeStruct(shape, jnp.float32), jax.ShapeDtypeStruct(shape, jnp.bfloat16)],
        in_specs=[IN_SMEM] + [IN_VMEM] * (len(misfits) + len(pieces) + 2),
        out_specs=[IN_VMEM] * 2,
        scratch_shapes=[pltpu.VMEM(tiles_of(pieces), jnp.bfloat16), pltpu.VMEM(shape, jnp.float32)],
        compiler_params=pltpu.CompilerParams(vmem_limit_bytes=SMALL_LIMIT),
        cost_estimate=LONG,
    )(words, *misfits, *pieces, factors, noise)


def coded_shape(per, tile, width):
    return jax.ShapeDtypeStruct((per * tile + SCALE_ROWS, width), jnp.int16)


def encode(blocks, out):
    per = len(blocks)
    tile, width = blocks[0].shape
    row = lax.broadcasted_iota(jnp.int32, (SCALE_ROWS, width), 0)
    powers = jnp.zeros((SCALE_ROWS, width), jnp.int32)
    for t, block in enumerate(blocks):
        largest = jnp.max(jnp.abs(block), axis=0, keepdims=True)
        power = jnp.ceil(SCALE_STEPS * jnp.log2(jnp.maximum(largest, 1e-20)))
        scaled = jnp.round(block * jnp.exp2(15.0 - power / SCALE_STEPS))
        out[pl.ds(t * tile, tile)] = jnp.clip(scaled, -32767.0, 32767.0).astype(jnp.int32).astype(jnp.int16)
        powers = jnp.where(row == t, power.astype(jnp.int32), powers)
    out[pl.ds(per * tile, SCALE_ROWS)] = powers.astype(jnp.int16)


def decoded(ref, t, tile, per):
    powers = ref[pl.ds(per * tile, SCALE_ROWS)].astype(jnp.int32).astype(jnp.float32)
    unit = jnp.exp2(powers[t : t + 1] / SCALE_STEPS - 15.0)
    return ref[pl.ds(t * tile, tile)].astype(jnp.int32).astype(jnp.float32) * unit


def join_kernel(count, mine, *refs):
    others = [ref[t] for ref in refs[:count] for t in range(ref.shape[0])]
    encode([mine[t] + other for t, other in enumerate(others)], refs[-1])


def join(mine, others, after):
    return pl.pallas_call(
        functools.partial(join_kernel, len(others)),
        out_shape=coded_shape(*mine.shape),
        in_specs=[IN_VMEM] * (1 + len(others)) + [ANY] * len(after),
        out_specs=IN_VMEM,
        compiler_params=pltpu.CompilerParams(vmem_limit_bytes=SMALL_LIMIT),
        cost_estimate=BRIEF,
    )(mine, *others, *after)


def owner_sum(mine, other, coded, t):
    per, tile, _ = mine.shape
    total = mine[t] + other[t]
    for ref in coded:
        total = total + decoded(ref, t, tile, per)
    return total


def update_kernel(power, mine, other, *refs):
    *coded, factors, noise, new, new_bf = refs
    for t in range(mine.shape[0]):
        step = HALF_STEP * power * owner_sum(mine, other, coded, t) + ROOT_STEP * noise[t].astype(jnp.float32)
        after = factors[t] - HALF_STEP * PRIOR * factors[t] + step
        new[t] = after
        new_bf[t] = after.astype(jnp.bfloat16)


def delta_kernel(power, mine, other, *refs):
    *coded, noise, out = refs
    steps = []
    for t in range(mine.shape[0]):
        steps.append(HALF_STEP * power * owner_sum(mine, other, coded, t) + ROOT_STEP * noise[t].astype(jnp.float32))
    encode(steps, out)


def arrive_kernel(coded, factors, new, new_bf):
    per, tile, _ = factors.shape
    for t in range(per):
        after = factors[t] - HALF_STEP * PRIOR * factors[t] + decoded(coded, t, tile, per)
        new[t] = after
        new_bf[t] = after.astype(jnp.bfloat16)


def pass_kernel(given, *refs):
    refs[-1][...] = given[...]


def in_vmem(kernel, out_shape, *operands, after=()):
    return pl.pallas_call(
        kernel,
        out_shape=out_shape,
        in_specs=[IN_VMEM] * len(operands) + [ANY] * len(after),
        out_specs=jax.tree.map(lambda _: IN_VMEM, out_shape),
        compiler_params=pltpu.CompilerParams(vmem_limit_bytes=SMALL_LIMIT),
        cost_estimate=BRIEF,
    )(*operands, *after)


def gathered(own, runs):
    evens = [own]
    for d in range(1, runs):
        relayed = runs == 4 and d == 3
        evens.append(swapped(evens[1] if relayed else own, "user", 4 if relayed else 2 * d))
    return evens


def body(u_factors, v_factors, ratings, tile_rows, tile_cols, tile_counts, u_noise, v_noise):
    tile = ratings.shape[-1]
    sections = ratings.shape[2]
    width = u_factors.shape[1]
    peers = lax.axis_size("user")
    power = float(lax.axis_size("item"))
    me = lax.axis_index("user").astype(jnp.int32).reshape(1)
    users = u_factors.reshape(-1, tile, width)
    items = v_factors.reshape(-1, tile, width)
    per = items.shape[0]
    item_tiles = peers * per
    span = 2 * per
    runs = item_tiles // span
    ratings = ratings.reshape(ratings.shape[2:])
    counts = tile_counts.reshape(sections)
    u_noise = u_noise.reshape(sections, *users.shape)
    v_noise = v_noise.reshape(sections, *items.shape)
    side = -(-ratings.shape[1] // 128) * 128
    assert (ratings.shape[1] + item_tiles) // 2 + runs * GROUP <= side - SCALARS and runs < SCALARS
    assert per & (per - 1) == 0
    bits = widths(ratings.shape[1], users.shape[0], item_tiles)
    pair = (
        jax.ShapeDtypeStruct(items.shape, jnp.float32),
        jax.ShapeDtypeStruct(items.shape, jnp.bfloat16),
    )
    rated = fetch(counts, ratings)
    items_bf = items.astype(jnp.bfloat16)
    users_bf = users.astype(jnp.bfloat16)
    for section in range(sections):
        words = pair_plan(section, bits, per, span, runs, side, me, counts, tile_rows, tile_cols)
        sent = items_bf
        if section:
            sent = shifted(items_bf, "item", section)
            sent = in_vmem(pass_kernel, jax.ShapeDtypeStruct(sent.shape, sent.dtype), sent, after=(users_bf, words))
        evens = gathered(sent, runs)
        chunks = [[even, swapped(even, "user", 1)] for even in evens]
        mine, other, sums, misfits = {}, {}, {}, {}
        after = [evens[2]]
        order = [(item_grads, run) for run in range(1, runs - 1)]
        order += [(join, run) for run in range(1, runs - 1)]
        order += [(item_grads, runs - 1), (item_grads, 0), (join, runs - 1)]
        for call, run in order:
            if call is item_grads:
                mine[run], odd_grads, misfits[run] = item_grads(
                    section, run, per, bits, words, rated, users_bf, chunks[run], after, 2 if run else 1
                )
                other[run] = [swapped(grad, "user", 1) for grad in odd_grads]
                after = [mine[run]]
            else:
                if run == runs - 1:
                    after += list(sums.values())
                after = [join(mine[run], other[run], after)]
                sums[run] = swapped(after[0], "user", 2 * run)
        sums = [sums[run] for run in range(1, runs)]
        misfits = [misfits[run] for run in range(runs)]
        pieces = [piece for chunk in chunks for piece in chunk]
        if section == 0:
            items, items_bf = in_vmem(
                functools.partial(update_kernel, power),
                pair,
                mine[0],
                other[0][0],
                *sums,
                items,
                v_noise[section],
            )
        else:
            delta = in_vmem(
                functools.partial(delta_kernel, power),
                coded_shape(*items.shape),
                mine[0],
                other[0][0],
                *sums,
                v_noise[section],
            )
            items, items_bf = in_vmem(arrive_kernel, pair, shifted(delta, "item", -section), items)
        users, users_bf = user_step(power, bits, words, misfits, pieces, users, u_noise[section])
    return (users.reshape(u_factors.shape), items.reshape(v_factors.shape))


def solution(mesh):
    placed = (
        P(("user", "item"), None),
        P(("item", "user"), None),
        P("user", "item", None, None, None, None),
        P("user", "item", None, None),
        P("user", "item", None, None),
        P("user", "item", None),
        P(None, ("user", "item"), None),
        P(None, ("item", "user"), None),
    )
    return jax.shard_map(
        body,
        mesh=mesh,
        in_specs=placed,
        out_specs=(P(("user", "item"), None), P(("item", "user"), None)),
        check_vma=False,
    )
```

```python
import functools
import math

import jax
import jax.numpy as jnp
from jax import lax
from jax.experimental import pallas as pl
from jax.experimental.pallas import tpu as pltpu
from jax.sharding import PartitionSpec as P

HALF_STEP = 0.002
ROOT_STEP = math.sqrt(0.004)
PRIOR = 25.0
GROUP = 4
SCALE_ROWS = 16
SMALL_LIMIT = 12 * 2**20
FETCH_LIMIT = 38 * 2**20
SCALE_STEPS = 128.0
SCALARS = 16
LONG = pl.CostEstimate(flops=4 * 10**9, bytes_accessed=2**12, transcendentals=0)
BRIEF = pl.CostEstimate(flops=10**8, bytes_accessed=2**12, transcendentals=0)

ANY = pl.BlockSpec(memory_space=pl.ANY)
IN_HBM = pl.BlockSpec(memory_space=pltpu.HBM)
IN_VMEM = pl.BlockSpec(memory_space=pltpu.VMEM)
IN_SMEM = pl.BlockSpec(memory_space=pltpu.SMEM)


def shifted(x, axis, by):
    peers = lax.axis_size(axis)
    return lax.ppermute(x, axis, [(i, (i + by) % peers) for i in range(peers)])


def swapped(x, axis, mask):
    peers = lax.axis_size(axis)
    return lax.ppermute(x, axis, [(i, i ^ mask) for i in range(peers)])


def widths(slots, user_tiles, item_tiles):
    bits = tuple(max(1, (n - 1).bit_length()) for n in (slots, user_tiles, item_tiles))
    assert 2 * bits[0] + 2 * bits[1] + bits[2] + 2 <= 31
    return bits


def total(x, axis):
    return jnp.sum(x.astype(jnp.float32), axis=axis, keepdims=True).astype(jnp.int32)


def plan_kernel(section, bits, per, span, runs, me, counts, rows, cols, words, lists):
    slot_bits, row_bits, col_bits = bits
    side = lists.shape[-1]
    slots = rows.shape[-1]
    shape = (side, side)
    count = counts[section]
    lists[...] = jnp.zeros_like(lists)
    lists[0:1, 0:slots] = rows[0, 0, section : section + 1]
    lists[1:2, 0:slots] = cols[0, 0, section : section + 1]
    along = lax.broadcasted_iota(jnp.int32, shape, 1)
    down = lax.broadcasted_iota(jnp.int32, shape, 0)
    row_along = jnp.broadcast_to(lists[0:1], shape)
    place_along = jnp.broadcast_to(lists[1:2] ^ (me[0] * per), shape)
    key = (place_along << row_bits | row_along).astype(jnp.float32).T.astype(jnp.int32)
    row_down = key & ((1 << row_bits) - 1)
    place_down = key >> row_bits
    span_bits = span.bit_length() - 1
    run_along, run_down = place_along >> span_bits, place_down >> span_bits
    live_along, live_down = along < count, down < count
    same = place_along == place_down
    rank_down = total(same & live_along & (row_along < row_down), 1)
    rank_along = total(same & live_down & (row_down < row_along), 0)
    opens = live_along & ((rank_along & 1) == 0)
    within = total(opens & (run_along == run_down) & (place_along < place_down), 1)
    base = jnp.zeros((side, 1), jnp.int32)
    begins = jnp.zeros((1, side), jnp.int32)
    unused = jnp.zeros((1, side), jnp.int32)
    ahead = jnp.zeros((1, 1), jnp.int32)
    for run in range(runs):
        size = total(opens[0:1] & (run_along[0:1] == run), 1)
        size = (size + GROUP - 1) & ~(GROUP - 1)
        base += jnp.where(run_down[:, 0:1] > run, size, 0)
        begins += jnp.where(along[0:1] > side - SCALARS + run, size, 0)
        ahead += size
        unused += jnp.where(along[0:1] >= ahead, span, 0)
    where = base + within + (rank_down >> 1)
    col_at = 2 * slot_bits + 2 * row_bits
    odd = rank_down & 1
    n, row, place = down[:, 0:1], row_down[:, 0:1], place_down[:, 0:1]
    word = jnp.where(odd == 0, n, n << slot_bits)
    word += jnp.where(odd == 0, row, row << row_bits) << (2 * slot_bits)
    word += (jnp.where(odd == 0, place, 0) << col_at) + (1 << (col_at + col_bits))
    word = jnp.broadcast_to(word, shape)
    hit = (where == along) & live_down
    low = total(jnp.where(hit, word & 0xFFFF, 0), 0)
    high = total(jnp.where(hit, word >> 16, 0), 0)
    listed = (high << 16) | low
    unused = jnp.minimum(unused, span * runs - 1) << col_at
    listed = jnp.where(listed == 0, unused, listed)
    words[...] = jnp.where(along[0:1] >= side - SCALARS, begins, listed)


def pair_plan(section, bits, per, span, runs, side, me, counts, rows, cols):
    return pl.pallas_call(
        functools.partial(plan_kernel, section, bits, per, span, runs),
        out_shape=jax.ShapeDtypeStruct((1, side), jnp.int32),
        in_specs=[IN_SMEM, IN_SMEM, IN_VMEM, IN_VMEM],
        out_specs=IN_VMEM,
        scratch_shapes=[pltpu.VMEM((8, side), jnp.int32)],
        compiler_params=pltpu.CompilerParams(vmem_limit_bytes=SMALL_LIMIT),
        cost_estimate=LONG,
    )(me, counts, rows, cols)


def bounds(words, run):
    at = words.shape[-1] - SCALARS + run
    return words[0, at], words[0, at + 1]


def decode_word(word, bits, first_col):
    slot_bits, row_bits, col_bits = bits
    fields = []
    for width in (slot_bits, slot_bits, row_bits, row_bits, col_bits):
        fields.append(word & ((1 << width) - 1))
        word = word >> width
    fields[4] -= first_col
    return (*fields, word)


def fetch_kernel(lump, counts, ratings, out, sem):
    def loads(section):
        def load(i):
            part = pl.ds(i * lump, lump)
            return pltpu.make_async_copy(ratings.at[section, part], out.at[section, part], sem.at[section, i])

        return lax.div(counts[section] + lump - 1, lump), load

    for section in range(ratings.shape[0]):
        lumps, load = loads(section)
        lax.fori_loop(0, lumps, lambda i, c, load=load: (load(i).start(), c)[1], 0)
    for section in range(ratings.shape[0]):
        lumps, load = loads(section)
        lax.fori_loop(0, lumps, lambda i, c, load=load: (load(i).wait(), c)[1], 0)


def fetch(counts, ratings):
    sections, slots = ratings.shape[:2]
    lump = math.gcd(slots, 16)
    return pl.pallas_call(
        functools.partial(fetch_kernel, lump),
        out_shape=jax.ShapeDtypeStruct(ratings.shape, ratings.dtype),
        in_specs=[IN_SMEM, IN_HBM],
        out_specs=IN_VMEM,
        scratch_shapes=[pltpu.SemaphoreType.DMA((sections, slots // lump))],
        compiler_params=pltpu.CompilerParams(vmem_limit_bytes=FETCH_LIMIT),
        cost_estimate=LONG,
    )(counts, ratings)


def gather_tiles(pieces, items):
    at = 0
    for piece in pieces:
        for t in range(piece.shape[0]):
            items[at + t] = piece[t]
        at += piece.shape[0]


def items_kernel(section, run, count, skipped, bits, listed, ratings, users, *refs):
    outs = refs[count + skipped : -4]
    items, grad, words, sem = refs[-4:]
    load = pltpu.make_async_copy(listed, words, sem)
    load.start()
    out_even, *out_odd, misfits = outs
    span = items.shape[0]
    per = span // 2
    tile = users.shape[1]
    gather_tiles(refs[:count], items)
    grad[...] = jnp.zeros_like(grad)
    load.wait()
    low, high = bounds(words, run)
    steps = lax.div(high - low, GROUP)

    def decode(p):
        return decode_word(words[0, p], bits, run * span)

    def users_of(row_a, row_b):
        return jnp.concatenate([users[row_a], users[row_b]], axis=0)

    def predict(p):
        slot_a, slot_b, row_a, row_b, col, live = decode(p)
        predicted = lax.dot_general(
            users_of(row_a, row_b), items[col], (((1,), (0,)), ((), ())), preferred_element_type=jnp.float32
        )
        given = jnp.concatenate([ratings[section, slot_a], ratings[section, slot_b]], axis=0).astype(jnp.float32)
        rows = lax.broadcasted_iota(jnp.int32, (2 * tile, 1), 0)
        return jnp.where(rows < tile * live, given - predicted, 0.0).astype(jnp.bfloat16)

    def add_grad(p, misfit):
        _, _, row_a, row_b, col, _ = decode(p)
        grad[col] += lax.dot_general(
            misfit, users_of(row_a, row_b), (((0,), (0,)), ((), ())), preferred_element_type=jnp.float32
        )

    @pl.when(steps > 0)
    def _():
        for j in range(GROUP):
            misfits[j] = predict(low + j)

        def advance(step, carry):
            at = step * GROUP
            held = [misfits[at + j] for j in range(GROUP)]
            following = [predict(low + at + GROUP + j) for j in range(GROUP)]
            for j in range(GROUP):
                add_grad(low + at + j, held[j])
            for j in range(GROUP):
                misfits[at + GROUP + j] = following[j]
            return carry

        lax.fori_loop(0, steps - 1, advance, 0)
        for j in range(GROUP):
            add_grad(high - GROUP + j, misfits[high - low - GROUP + j])

    at = 0
    for out in (out_even, *out_odd):
        for t in range(out.shape[0]):
            out[t] = grad[at + t]
        at += out.shape[0]


def item_grads(section, run, per, bits, words, ratings, users, pieces, after, parts):
    tile, width = users.shape[1:]
    f32 = jnp.float32
    held = per * (users.shape[0] + users.shape[0] % 2)
    held = -(-min(held, ratings.shape[1] // 2 + per) // GROUP) * GROUP
    even_grad, *odd_grads, misfits = pl.pallas_call(
        functools.partial(items_kernel, section, run, len(pieces), len(after), bits),
        out_shape=[jax.ShapeDtypeStruct((per, tile, width), f32)]
        + [jax.ShapeDtypeStruct((per // parts, tile, width), f32)] * parts
        + [jax.ShapeDtypeStruct((held, 2 * tile, tile), jnp.bfloat16)],
        in_specs=[ANY] + [IN_VMEM] * (2 + len(pieces)) + [ANY] * len(after),
        out_specs=[IN_VMEM] * (2 + parts),
        scratch_shapes=[
            pltpu.VMEM((2 * per, width, tile), jnp.bfloat16),
            pltpu.VMEM((2 * per, tile, width), f32),
            pltpu.SMEM(words.shape, jnp.int32),
            pltpu.SemaphoreType.DMA,
        ],
        compiler_params=pltpu.CompilerParams(vmem_limit_bytes=SMALL_LIMIT),
        cost_estimate=LONG,
    )(words, ratings, users, *pieces, *after)
    return even_grad, odd_grads, misfits


def add_user_grads(bits, first_run, words, pieces, misfits, items, grad):
    tile = grad.shape[1]
    first_col = first_run * items.shape[0] // len(misfits)
    gather_tiles(pieces, items)
    for run, held in enumerate(misfits, first_run):
        low, high = bounds(words, run)

        def advance(step, carry, low=low, held=held):
            for j in range(GROUP):
                at = step * GROUP + j
                _, _, row_a, row_b, col, _ = decode_word(words[0, low + at], bits, first_col)
                part = lax.dot_general(
                    held[at], items[col], (((1,), (1,)), ((), ())), preferred_element_type=jnp.float32
                )
                grad[row_a] += part[:tile]
                grad[row_b] += part[tile:]
            return carry

        lax.fori_loop(0, lax.div(high - low, GROUP), advance, 0)


def users_head_kernel(bits, runs, words, *refs):
    *pieces, grad, items = refs[runs:]
    grad[...] = jnp.zeros_like(grad)
    add_user_grads(bits, 0, words, pieces, refs[:runs], items, grad)


def users_tail_kernel(power, bits, first_run, words, held, *refs):
    *pieces, factors, noise, partial, new, new_bf, items, grad = refs
    grad[...] = partial[...]
    add_user_grads(bits, first_run, words, pieces, [held], items, grad)

    def finish(t, carry):
        before = factors[t]
        after = (
            before + HALF_STEP * (power * grad[t] - PRIOR * before) + ROOT_STEP * noise[t].astype(jnp.float32)
        )
        new[t] = after
        new_bf[t] = after.astype(jnp.bfloat16)
        return carry

    lax.fori_loop(0, factors.shape[0], finish, 0)


def tiles_of(pieces):
    return sum(piece.shape[0] for piece in pieces), *pieces[0].shape[1:]


def users_head(bits, words, misfits, pieces, shape):
    return pl.pallas_call(
        functools.partial(users_head_kernel, bits, len(misfits)),
        out_shape=jax.ShapeDtypeStruct(shape, jnp.float32),
        in_specs=[IN_SMEM] + [IN_VMEM] * (len(misfits) + len(pieces)),
        out_specs=IN_VMEM,
        scratch_shapes=[pltpu.VMEM(tiles_of(pieces), jnp.bfloat16)],
        compiler_params=pltpu.CompilerParams(vmem_limit_bytes=SMALL_LIMIT),
        cost_estimate=BRIEF,
    )(words, *misfits, *pieces)


def users_tail(power, bits, first_run, words, misfits, pieces, factors, noise, partial):
    shape = factors.shape
    return pl.pallas_call(
        functools.partial(users_tail_kernel, power, bits, first_run),
        out_shape=[jax.ShapeDtypeStruct(shape, jnp.float32), jax.ShapeDtypeStruct(shape, jnp.bfloat16)],
        in_specs=[IN_SMEM, IN_VMEM] + [IN_VMEM] * (len(pieces) + 3),
        out_specs=[IN_VMEM] * 2,
        scratch_shapes=[pltpu.VMEM(tiles_of(pieces), jnp.bfloat16), pltpu.VMEM(shape, jnp.float32)],
        compiler_params=pltpu.CompilerParams(vmem_limit_bytes=SMALL_LIMIT),
        cost_estimate=BRIEF,
    )(words, misfits, *pieces, factors, noise, partial)


def coded_shape(per, tile, width):
    return jax.ShapeDtypeStruct((per * tile + SCALE_ROWS, width), jnp.int16)


def encode(blocks, out):
    per = len(blocks)
    tile, width = blocks[0].shape
    row = lax.broadcasted_iota(jnp.int32, (SCALE_ROWS, width), 0)
    powers = jnp.zeros((SCALE_ROWS, width), jnp.int32)
    for t, block in enumerate(blocks):
        largest = jnp.max(jnp.abs(block), axis=0, keepdims=True)
        power = jnp.ceil(SCALE_STEPS * jnp.log2(jnp.maximum(largest, 1e-20)))
        scaled = jnp.round(block * jnp.exp2(15.0 - power / SCALE_STEPS))
        out[pl.ds(t * tile, tile)] = jnp.clip(scaled, -32767.0, 32767.0).astype(jnp.int32).astype(jnp.int16)
        powers = jnp.where(row == t, power.astype(jnp.int32), powers)
    out[pl.ds(per * tile, SCALE_ROWS)] = powers.astype(jnp.int16)


def decoded(ref, t, tile, per):
    powers = ref[pl.ds(per * tile, SCALE_ROWS)].astype(jnp.int32).astype(jnp.float32)
    unit = jnp.exp2(powers[t : t + 1] / SCALE_STEPS - 15.0)
    return ref[pl.ds(t * tile, tile)].astype(jnp.int32).astype(jnp.float32) * unit


def join_kernel(count, mine, *refs):
    others = [ref[t] for ref in refs[:count] for t in range(ref.shape[0])]
    encode([mine[t] + other for t, other in enumerate(others)], refs[-1])


def join(mine, others, after):
    return pl.pallas_call(
        functools.partial(join_kernel, len(others)),
        out_shape=coded_shape(*mine.shape),
        in_specs=[IN_VMEM] * (1 + len(others)) + [ANY] * len(after),
        out_specs=IN_VMEM,
        compiler_params=pltpu.CompilerParams(vmem_limit_bytes=SMALL_LIMIT),
        cost_estimate=BRIEF,
    )(mine, *others, *after)


def owner_sum(mine, other, coded, t):
    per, tile, _ = mine.shape
    total = mine[t] + other[t]
    for ref in coded:
        total = total + decoded(ref, t, tile, per)
    return total


def update_kernel(power, mine, other, *refs):
    *coded, factors, noise, _, new, new_bf = refs
    for t in range(mine.shape[0]):
        step = HALF_STEP * power * owner_sum(mine, other, coded, t) + ROOT_STEP * noise[t].astype(jnp.float32)
        after = factors[t] - HALF_STEP * PRIOR * factors[t] + step
        new[t] = after
        new_bf[t] = after.astype(jnp.bfloat16).T


def delta_kernel(power, mine, other, *refs):
    *coded, noise, _, out = refs
    steps = []
    for t in range(mine.shape[0]):
        steps.append(HALF_STEP * power * owner_sum(mine, other, coded, t) + ROOT_STEP * noise[t].astype(jnp.float32))
    encode(steps, out)


def arrive_kernel(coded, factors, new, *new_bf):
    per, tile, _ = factors.shape
    for t in range(per):
        after = factors[t] - HALF_STEP * PRIOR * factors[t] + decoded(coded, t, tile, per)
        new[t] = after
        for out in new_bf:
            out[t] = after.astype(jnp.bfloat16).T


def turn_kernel(factors, out):
    for t in range(factors.shape[0]):
        out[t] = factors[t].astype(jnp.bfloat16).T


def pass_kernel(given, *refs):
    refs[-1][...] = given[...]


def in_vmem(kernel, out_shape, *operands, after=()):
    return pl.pallas_call(
        kernel,
        out_shape=out_shape,
        in_specs=[IN_VMEM] * len(operands) + [ANY] * len(after),
        out_specs=jax.tree.map(lambda _: IN_VMEM, out_shape),
        compiler_params=pltpu.CompilerParams(vmem_limit_bytes=SMALL_LIMIT),
        cost_estimate=BRIEF,
    )(*operands, *after)


def gathered(own, runs):
    evens = [own]
    for d in range(1, runs):
        relayed = runs == 4 and d == 3
        evens.append(swapped(evens[1] if relayed else own, "user", 4 if relayed else 2 * d))
    return evens


def body(u_factors, v_factors, ratings, tile_rows, tile_cols, tile_counts, u_noise, v_noise):
    tile = ratings.shape[-1]
    sections = ratings.shape[2]
    width = u_factors.shape[1]
    peers = lax.axis_size("user")
    power = float(lax.axis_size("item"))
    me = lax.axis_index("user").astype(jnp.int32).reshape(1)
    users = u_factors.reshape(-1, tile, width)
    items = v_factors.reshape(-1, tile, width)
    per = items.shape[0]
    item_tiles = peers * per
    span = 2 * per
    runs = item_tiles // span
    ratings = ratings.reshape(ratings.shape[2:])
    counts = tile_counts.reshape(sections)
    u_noise = u_noise.reshape(sections, *users.shape)
    v_noise = v_noise.reshape(sections, *items.shape)
    side = -(-ratings.shape[1] // 128) * 128
    assert (ratings.shape[1] + item_tiles) // 2 + runs * GROUP <= side - SCALARS and runs < SCALARS
    assert per & (per - 1) == 0
    bits = widths(ratings.shape[1], users.shape[0], item_tiles)
    pair = (
        jax.ShapeDtypeStruct(items.shape, jnp.float32),
        jax.ShapeDtypeStruct((per, width, tile), jnp.bfloat16),
    )
    rated = fetch(counts, ratings)
    items_bf = in_vmem(turn_kernel, pair[1], items)
    users_bf = users.astype(jnp.bfloat16)
    for section in range(sections):
        words = pair_plan(section, bits, per, span, runs, side, me, counts, tile_rows, tile_cols)
        sent = items_bf
        if section:
            sent = shifted(items_bf, "item", section)
            sent = in_vmem(pass_kernel, jax.ShapeDtypeStruct(sent.shape, sent.dtype), sent, after=(users_bf, words))
        evens = gathered(sent, runs)
        chunks = [[even, swapped(even, "user", 1)] for even in evens]
        mine, other, sums, misfits = {}, {}, {}, {}
        after = [evens[2]]
        order = [(item_grads, run) for run in range(1, runs - 1)]
        order += [(join, run) for run in range(1, runs - 1)]
        order += [(item_grads, runs - 1), (item_grads, 0), (join, runs - 1)]
        for call, run in order:
            if call is item_grads:
                mine[run], odd_grads, misfits[run] = item_grads(
                    section, run, per, bits, words, rated, users_bf, chunks[run], after, 2 if run else 1
                )
                other[run] = [swapped(grad, "user", 1) for grad in odd_grads]
                after = [mine[run]]
            else:
                if run == runs - 1:
                    after += list(sums.values())
                after = [join(mine[run], other[run], after)]
                sums[run] = swapped(after[0], "user", 2 * run)
        sums = [sums[run] for run in range(1, runs)]
        misfits = [misfits[run] for run in range(runs)]
        head = [piece for chunk in chunks[:-1] for piece in chunk]
        partial = users_head(bits, words, misfits[:-1], head, users.shape)
        if section == 0:
            items, items_bf = in_vmem(
                functools.partial(update_kernel, power),
                pair,
                mine[0],
                other[0][0],
                *sums,
                items,
                v_noise[section],
                after=(partial,),
            )
        else:
            delta = in_vmem(
                functools.partial(delta_kernel, power),
                coded_shape(*items.shape),
                mine[0],
                other[0][0],
                *sums,
                v_noise[section],
                after=(partial,),
            )
            wanted = pair if section + 1 < sections else pair[:1]
            items, *turned = in_vmem(arrive_kernel, wanted, shifted(delta, "item", -section), items)
            items_bf = turned[0] if turned else None
        users, users_bf = users_tail(
            power, bits, runs - 1, words, misfits[-1], chunks[-1], users, u_noise[section], partial
        )
    return (users.reshape(u_factors.shape), items.reshape(v_factors.shape))


def solution(mesh):
    placed = (
        P(("user", "item"), None),
        P(("item", "user"), None),
        P("user", "item", None, None, None, None),
        P("user", "item", None, None),
        P("user", "item", None, None),
        P("user", "item", None),
        P(None, ("user", "item"), None),
        P(None, ("item", "user"), None),
    )
    return jax.shard_map(
        body,
        mesh=mesh,
        in_specs=placed,
        out_specs=(P(("user", "item"), None), P(("item", "user"), None)),
        check_vma=False,
    )
```

```python
import functools
import math

import jax
import jax.numpy as jnp
from jax import lax
from jax.experimental import pallas as pl
from jax.experimental.pallas import tpu as pltpu
from jax.sharding import PartitionSpec as P

HALF_STEP = 0.002
ROOT_STEP = math.sqrt(0.004)
PRIOR = 25.0
GROUP = 4
SCALE_ROWS = 16
SMALL_LIMIT = 12 * 2**20
FETCH_LIMIT = 38 * 2**20
SCALE_STEPS = 128.0
SCALARS = 16
LONG = pl.CostEstimate(flops=4 * 10**9, bytes_accessed=2**12, transcendentals=0)
BRIEF = pl.CostEstimate(flops=10**8, bytes_accessed=2**12, transcendentals=0)

ANY = pl.BlockSpec(memory_space=pl.ANY)
IN_HBM = pl.BlockSpec(memory_space=pltpu.HBM)
IN_VMEM = pl.BlockSpec(memory_space=pltpu.VMEM)
IN_SMEM = pl.BlockSpec(memory_space=pltpu.SMEM)


def shifted(x, axis, by):
    peers = lax.axis_size(axis)
    return lax.ppermute(x, axis, [(i, (i + by) % peers) for i in range(peers)])


def swapped(x, axis, mask):
    peers = lax.axis_size(axis)
    return lax.ppermute(x, axis, [(i, i ^ mask) for i in range(peers)])


def widths(slots, user_tiles, item_tiles):
    bits = tuple(max(1, (n - 1).bit_length()) for n in (slots, user_tiles, item_tiles))
    assert 2 * bits[0] + 2 * bits[1] + bits[2] + 2 <= 31
    return bits


def total(x, axis):
    return jnp.sum(x.astype(jnp.float32), axis=axis, keepdims=True).astype(jnp.int32)


def plan_kernel(section, bits, per, span, runs, me, counts, rows, cols, words, lists):
    slot_bits, row_bits, col_bits = bits
    side = lists.shape[-1]
    slots = rows.shape[-1]
    shape = (side, side)
    count = counts[section]
    lists[...] = jnp.zeros_like(lists)
    lists[0:1, 0:slots] = rows[0, 0, section : section + 1]
    lists[1:2, 0:slots] = cols[0, 0, section : section + 1]
    along = lax.broadcasted_iota(jnp.int32, shape, 1)
    down = lax.broadcasted_iota(jnp.int32, shape, 0)
    row_along = jnp.broadcast_to(lists[0:1], shape)
    place_along = jnp.broadcast_to(lists[1:2] ^ (me[0] * per), shape)
    key = (place_along << row_bits | row_along).astype(jnp.float32).T.astype(jnp.int32)
    row_down = key & ((1 << row_bits) - 1)
    place_down = key >> row_bits
    span_bits = span.bit_length() - 1
    run_along, run_down = place_along >> span_bits, place_down >> span_bits
    live_along, live_down = along < count, down < count
    same = place_along == place_down
    rank_down = total(same & live_along & (row_along < row_down), 1)
    rank_along = total(same & live_down & (row_down < row_along), 0)
    opens = live_along & ((rank_along & 1) == 0)
    within = total(opens & (run_along == run_down) & (place_along < place_down), 1)
    base = jnp.zeros((side, 1), jnp.int32)
    begins = jnp.zeros((1, side), jnp.int32)
    unused = jnp.zeros((1, side), jnp.int32)
    ahead = jnp.zeros((1, 1), jnp.int32)
    for run in range(runs):
        size = total(opens[0:1] & (run_along[0:1] == run), 1)
        size = (size + GROUP - 1) & ~(GROUP - 1)
        base += jnp.where(run_down[:, 0:1] > run, size, 0)
        begins += jnp.where(along[0:1] > side - SCALARS + run, size, 0)
        ahead += size
        unused += jnp.where(along[0:1] >= ahead, span, 0)
    where = base + within + (rank_down >> 1)
    col_at = 2 * slot_bits + 2 * row_bits
    odd = rank_down & 1
    n, row, place = down[:, 0:1], row_down[:, 0:1], place_down[:, 0:1]
    word = jnp.where(odd == 0, n, n << slot_bits)
    word += jnp.where(odd == 0, row, row << row_bits) << (2 * slot_bits)
    word += (jnp.where(odd == 0, place, 0) << col_at) + (1 << (col_at + col_bits))
    word = jnp.broadcast_to(word, shape)
    hit = (where == along) & live_down
    low = total(jnp.where(hit, word & 0xFFFF, 0), 0)
    high = total(jnp.where(hit, word >> 16, 0), 0)
    listed = (high << 16) | low
    unused = jnp.minimum(unused, span * runs - 1) << col_at
    listed = jnp.where(listed == 0, unused, listed)
    words[...] = jnp.where(along[0:1] >= side - SCALARS, begins, listed)


def pair_plan(section, bits, per, span, runs, side, me, counts, rows, cols):
    return pl.pallas_call(
        functools.partial(plan_kernel, section, bits, per, span, runs),
        out_shape=jax.ShapeDtypeStruct((1, side), jnp.int32),
        in_specs=[IN_SMEM, IN_SMEM, IN_VMEM, IN_VMEM],
        out_specs=IN_VMEM,
        scratch_shapes=[pltpu.VMEM((8, side), jnp.int32)],
        compiler_params=pltpu.CompilerParams(vmem_limit_bytes=SMALL_LIMIT),
        cost_estimate=LONG,
    )(me, counts, rows, cols)


def bounds(words, run):
    at = words.shape[-1] - SCALARS + run
    return words[0, at], words[0, at + 1]


def decode_word(word, bits, first_col):
    slot_bits, row_bits, col_bits = bits
    fields = []
    for width in (slot_bits, slot_bits, row_bits, row_bits, col_bits):
        fields.append(word & ((1 << width) - 1))
        word = word >> width
    fields[4] -= first_col
    return (*fields, word)


def fetch_kernel(lump, counts, ratings, out, sem):
    def loads(section):
        def load(i):
            part = pl.ds(i * lump, lump)
            return pltpu.make_async_copy(ratings.at[section, part], out.at[section, part], sem.at[section, i])

        return lax.div(counts[section] + lump - 1, lump), load

    for section in range(ratings.shape[0]):
        lumps, load = loads(section)
        lax.fori_loop(0, lumps, lambda i, c, load=load: (load(i).start(), c)[1], 0)
    for section in range(ratings.shape[0]):
        lumps, load = loads(section)
        lax.fori_loop(0, lumps, lambda i, c, load=load: (load(i).wait(), c)[1], 0)


def fetch(counts, ratings):
    sections, slots = ratings.shape[:2]
    lump = math.gcd(slots, 16)
    return pl.pallas_call(
        functools.partial(fetch_kernel, lump),
        out_shape=jax.ShapeDtypeStruct(ratings.shape, ratings.dtype),
        in_specs=[IN_SMEM, IN_HBM],
        out_specs=IN_VMEM,
        scratch_shapes=[pltpu.SemaphoreType.DMA((sections, slots // lump))],
        compiler_params=pltpu.CompilerParams(vmem_limit_bytes=FETCH_LIMIT),
        cost_estimate=LONG,
    )(counts, ratings)


def gather_tiles(pieces, items):
    at = 0
    for piece in pieces:
        for t in range(piece.shape[0]):
            items[at + t] = piece[t]
        at += piece.shape[0]


def items_kernel(section, run, count, skipped, bits, listed, ratings, users, *refs):
    outs = refs[count + skipped : -4]
    items, grad, words, sem = refs[-4:]
    load = pltpu.make_async_copy(listed, words, sem)
    load.start()
    out_even, *out_odd, misfits = outs
    span = items.shape[0]
    per = span // 2
    tile = users.shape[1]
    gather_tiles(refs[:count], items)
    grad[...] = jnp.zeros_like(grad)
    load.wait()
    low, high = bounds(words, run)
    steps = lax.div(high - low, GROUP)

    def decode(p):
        return decode_word(words[0, p], bits, run * span)

    def users_of(row_a, row_b):
        return jnp.concatenate([users[row_a], users[row_b]], axis=0)

    def predict(p):
        slot_a, slot_b, row_a, row_b, col, live = decode(p)
        predicted = lax.dot_general(
            users_of(row_a, row_b), items[col], (((1,), (0,)), ((), ())), preferred_element_type=jnp.float32
        )
        given = jnp.concatenate([ratings[section, slot_a], ratings[section, slot_b]], axis=0).astype(jnp.float32)
        rows = lax.broadcasted_iota(jnp.int32, (2 * tile, 1), 0)
        return jnp.where(rows < tile * live, given - predicted, 0.0).astype(jnp.bfloat16)

    def add_grad(p, misfit):
        _, _, row_a, row_b, col, _ = decode(p)
        grad[col] += lax.dot_general(
            misfit, users_of(row_a, row_b), (((0,), (0,)), ((), ())), preferred_element_type=jnp.float32
        )

    @pl.when(steps > 0)
    def _():
        for j in range(GROUP):
            misfits[j] = predict(low + j)

        def advance(step, carry):
            at = step * GROUP
            held = [misfits[at + j] for j in range(GROUP)]
            following = [predict(low + at + GROUP + j) for j in range(GROUP)]
            for j in range(GROUP):
                add_grad(low + at + j, held[j])
            for j in range(GROUP):
                misfits[at + GROUP + j] = following[j]
            return carry

        lax.fori_loop(0, steps - 1, advance, 0)
        for j in range(GROUP):
            add_grad(high - GROUP + j, misfits[high - low - GROUP + j])

    at = 0
    for out in (out_even, *out_odd):
        for t in range(out.shape[0]):
            out[t] = grad[at + t]
        at += out.shape[0]


def item_grads(section, run, per, bits, words, ratings, users, pieces, after, parts):
    tile, width = users.shape[1:]
    f32 = jnp.float32
    held = per * (users.shape[0] + users.shape[0] % 2)
    held = -(-min(held, ratings.shape[1] // 2 + per) // GROUP) * GROUP
    even_grad, *odd_grads, misfits = pl.pallas_call(
        functools.partial(items_kernel, section, run, len(pieces), len(after), bits),
        out_shape=[jax.ShapeDtypeStruct((per, tile, width), f32)]
        + [jax.ShapeDtypeStruct((per // parts, tile, width), f32)] * parts
        + [jax.ShapeDtypeStruct((held, 2 * tile, tile), jnp.bfloat16)],
        in_specs=[ANY] + [IN_VMEM] * (2 + len(pieces)) + [ANY] * len(after),
        out_specs=[IN_VMEM] * (2 + parts),
        scratch_shapes=[
            pltpu.VMEM((2 * per, width, tile), jnp.bfloat16),
            pltpu.VMEM((2 * per, tile, width), f32),
            pltpu.SMEM(words.shape, jnp.int32),
            pltpu.SemaphoreType.DMA,
        ],
        compiler_params=pltpu.CompilerParams(vmem_limit_bytes=SMALL_LIMIT),
        cost_estimate=LONG,
    )(words, ratings, users, *pieces, *after)
    return even_grad, odd_grads, misfits


def add_user_grads(bits, first_run, words, pieces, misfits, items, grad):
    tile = grad.shape[1]
    first_col = first_run * items.shape[0] // len(misfits)
    gather_tiles(pieces, items)
    for run, held in enumerate(misfits, first_run):
        low, high = bounds(words, run)

        def advance(step, carry, low=low, held=held):
            for j in range(GROUP):
                at = step * GROUP + j
                _, _, row_a, row_b, col, _ = decode_word(words[0, low + at], bits, first_col)
                part = lax.dot_general(
                    held[at], items[col], (((1,), (1,)), ((), ())), preferred_element_type=jnp.float32
                )
                grad[row_a] += part[:tile]
                grad[row_b] += part[tile:]
            return carry

        lax.fori_loop(0, lax.div(high - low, GROUP), advance, 0)


def users_head_kernel(bits, runs, words, *refs):
    *pieces, grad, items = refs[runs:]
    grad[...] = jnp.zeros_like(grad)
    add_user_grads(bits, 0, words, pieces, refs[:runs], items, grad)


def users_tail_kernel(power, bits, first_run, more, words, held, *refs):
    *pieces, factors, noise, partial = refs[: -3 - more]
    new, *new_bf = refs[-3 - more : -2]
    items, grad = refs[-2:]
    grad[...] = partial[...]
    add_user_grads(bits, first_run, words, pieces, [held], items, grad)

    def finish(t, carry):
        before = factors[t]
        after = (
            before + HALF_STEP * (power * grad[t] - PRIOR * before) + ROOT_STEP * noise[t].astype(jnp.float32)
        )
        new[t] = after
        for out in new_bf:
            out[t] = after.astype(jnp.bfloat16)
        return carry

    lax.fori_loop(0, factors.shape[0], finish, 0)


def tiles_of(pieces):
    return sum(piece.shape[0] for piece in pieces), *pieces[0].shape[1:]


def users_head(bits, words, misfits, pieces, shape):
    return pl.pallas_call(
        functools.partial(users_head_kernel, bits, len(misfits)),
        out_shape=jax.ShapeDtypeStruct(shape, jnp.float32),
        in_specs=[IN_SMEM] + [IN_VMEM] * (len(misfits) + len(pieces)),
        out_specs=IN_VMEM,
        scratch_shapes=[pltpu.VMEM(tiles_of(pieces), jnp.bfloat16)],
        compiler_params=pltpu.CompilerParams(vmem_limit_bytes=SMALL_LIMIT),
        cost_estimate=BRIEF,
    )(words, *misfits, *pieces)


def users_tail(power, bits, first_run, words, misfits, pieces, factors, noise, partial, more):
    shape = factors.shape
    return pl.pallas_call(
        functools.partial(users_tail_kernel, power, bits, first_run, more),
        out_shape=[jax.ShapeDtypeStruct(shape, jnp.float32), jax.ShapeDtypeStruct(shape, jnp.bfloat16)][: 1 + more],
        in_specs=[IN_SMEM, IN_VMEM] + [IN_VMEM] * (len(pieces) + 3),
        out_specs=[IN_VMEM] * (1 + more),
        scratch_shapes=[pltpu.VMEM(tiles_of(pieces), jnp.bfloat16), pltpu.VMEM(shape, jnp.float32)],
        compiler_params=pltpu.CompilerParams(vmem_limit_bytes=SMALL_LIMIT),
        cost_estimate=BRIEF,
    )(words, misfits, *pieces, factors, noise, partial)


def coded_shape(per, tile, width):
    return jax.ShapeDtypeStruct((per * tile + SCALE_ROWS, width), jnp.int16)


def encode(blocks, out):
    per = len(blocks)
    tile, width = blocks[0].shape
    row = lax.broadcasted_iota(jnp.int32, (SCALE_ROWS, width), 0)
    powers = jnp.zeros((SCALE_ROWS, width), jnp.int32)
    for t, block in enumerate(blocks):
        largest = jnp.max(jnp.abs(block), axis=0, keepdims=True)
        power = jnp.ceil(SCALE_STEPS * jnp.log2(jnp.maximum(largest, 1e-20)))
        scaled = jnp.round(block * jnp.exp2(15.0 - power / SCALE_STEPS))
        out[pl.ds(t * tile, tile)] = jnp.clip(scaled, -32767.0, 32767.0).astype(jnp.int32).astype(jnp.int16)
        powers = jnp.where(row == t, power.astype(jnp.int32), powers)
    out[pl.ds(per * tile, SCALE_ROWS)] = powers.astype(jnp.int16)


def decoded(ref, t, tile, per):
    powers = ref[pl.ds(per * tile, SCALE_ROWS)].astype(jnp.int32).astype(jnp.float32)
    unit = jnp.exp2(powers[t : t + 1] / SCALE_STEPS - 15.0)
    return ref[pl.ds(t * tile, tile)].astype(jnp.int32).astype(jnp.float32) * unit


def join_kernel(count, mine, *refs):
    others = [ref[t] for ref in refs[:count] for t in range(ref.shape[0])]
    encode([mine[t] + other for t, other in enumerate(others)], refs[-1])


def join(mine, others, after):
    return pl.pallas_call(
        functools.partial(join_kernel, len(others)),
        out_shape=coded_shape(*mine.shape),
        in_specs=[IN_VMEM] * (1 + len(others)) + [ANY] * len(after),
        out_specs=IN_VMEM,
        compiler_params=pltpu.CompilerParams(vmem_limit_bytes=SMALL_LIMIT),
        cost_estimate=BRIEF,
    )(mine, *others, *after)


def owner_sum(mine, other, coded, t):
    per, tile, _ = mine.shape
    total = mine[t] + other[t]
    for ref in coded:
        total = total + decoded(ref, t, tile, per)
    return total


def update_kernel(power, mine, other, *refs):
    *coded, factors, noise, _, new, new_bf = refs
    for t in range(mine.shape[0]):
        step = HALF_STEP * power * owner_sum(mine, other, coded, t) + ROOT_STEP * noise[t].astype(jnp.float32)
        after = factors[t] - HALF_STEP * PRIOR * factors[t] + step
        new[t] = after
        new_bf[t] = after.astype(jnp.bfloat16).T


def delta_kernel(power, mine, other, *refs):
    *coded, noise, _, out = refs
    steps = []
    for t in range(mine.shape[0]):
        steps.append(HALF_STEP * power * owner_sum(mine, other, coded, t) + ROOT_STEP * noise[t].astype(jnp.float32))
    encode(steps, out)


def arrive_kernel(coded, factors, new, *new_bf):
    per, tile, _ = factors.shape
    for t in range(per):
        after = factors[t] - HALF_STEP * PRIOR * factors[t] + decoded(coded, t, tile, per)
        new[t] = after
        for out in new_bf:
            out[t] = after.astype(jnp.bfloat16).T


def turn_kernel(factors, out):
    for t in range(factors.shape[0]):
        out[t] = factors[t].astype(jnp.bfloat16).T


def pass_kernel(given, *refs):
    refs[-1][...] = given[...]


def in_vmem(kernel, out_shape, *operands, after=()):
    return pl.pallas_call(
        kernel,
        out_shape=out_shape,
        in_specs=[IN_VMEM] * len(operands) + [ANY] * len(after),
        out_specs=jax.tree.map(lambda _: IN_VMEM, out_shape),
        compiler_params=pltpu.CompilerParams(vmem_limit_bytes=SMALL_LIMIT),
        cost_estimate=BRIEF,
    )(*operands, *after)


def gathered(own, runs, after):
    evens = [own]
    for d in range(1, runs):
        relayed = runs == 4 and d == 3
        evens.append(swapped(evens[1] if relayed else own, "user", 4 if relayed else 2 * d))
        if d == 1 and after:
            evens[1] = in_vmem(pass_kernel, jax.ShapeDtypeStruct(own.shape, own.dtype), evens[1], after=after)
    return evens


def body(u_factors, v_factors, ratings, tile_rows, tile_cols, tile_counts, u_noise, v_noise):
    tile = ratings.shape[-1]
    sections = ratings.shape[2]
    width = u_factors.shape[1]
    peers = lax.axis_size("user")
    power = float(lax.axis_size("item"))
    me = lax.axis_index("user").astype(jnp.int32).reshape(1)
    users = u_factors.reshape(-1, tile, width)
    items = v_factors.reshape(-1, tile, width)
    per = items.shape[0]
    item_tiles = peers * per
    span = 2 * per
    runs = item_tiles // span
    ratings = ratings.reshape(ratings.shape[2:])
    counts = tile_counts.reshape(sections)
    u_noise = u_noise.reshape(sections, *users.shape)
    v_noise = v_noise.reshape(sections, *items.shape)
    side = -(-ratings.shape[1] // 128) * 128
    assert (ratings.shape[1] + item_tiles) // 2 + runs * GROUP <= side - SCALARS and runs < SCALARS
    assert per & (per - 1) == 0
    bits = widths(ratings.shape[1], users.shape[0], item_tiles)
    pair = (
        jax.ShapeDtypeStruct(items.shape, jnp.float32),
        jax.ShapeDtypeStruct((per, width, tile), jnp.bfloat16),
    )
    rated = fetch(counts, ratings)
    items_bf = in_vmem(turn_kernel, pair[1], items)
    users_bf = users.astype(jnp.bfloat16)
    for section in range(sections):
        words = pair_plan(section, bits, per, span, runs, side, me, counts, tile_rows, tile_cols)
        sent = items_bf
        if section:
            sent = shifted(items_bf, "item", section)
            sent = in_vmem(pass_kernel, jax.ShapeDtypeStruct(sent.shape, sent.dtype), sent, after=(users_bf, words))
        evens = gathered(sent, runs, () if section else (words, rated))
        chunks = [[even, swapped(even, "user", 1)] for even in evens]
        mine, other, sums, misfits = {}, {}, {}, {}
        after = [evens[2]]
        order = [(item_grads, run) for run in range(1, runs - 1)]
        order += [(join, run) for run in range(1, runs - 1)]
        order += [(item_grads, runs - 1), (item_grads, 0), (join, runs - 1)]
        for call, run in order:
            if call is item_grads:
                mine[run], odd_grads, misfits[run] = item_grads(
                    section, run, per, bits, words, rated, users_bf, chunks[run], after, 2 if run else 1
                )
                other[run] = [swapped(grad, "user", 1) for grad in odd_grads]
                after = [mine[run]]
            else:
                if run == runs - 1:
                    after += list(sums.values())
                after = [join(mine[run], other[run], after)]
                sums[run] = swapped(after[0], "user", 2 * run)
        sums = [sums[run] for run in range(1, runs)]
        misfits = [misfits[run] for run in range(runs)]
        head = [piece for chunk in chunks[:-1] for piece in chunk]
        partial = users_head(bits, words, misfits[:-1], head, users.shape)
        if section == 0:
            items, items_bf = in_vmem(
                functools.partial(update_kernel, power),
                pair,
                mine[0],
                other[0][0],
                *sums,
                items,
                v_noise[section],
                after=(partial,),
            )
        else:
            delta = in_vmem(
                functools.partial(delta_kernel, power),
                coded_shape(*items.shape),
                mine[0],
                other[0][0],
                *sums,
                v_noise[section],
                after=(partial,),
            )
            wanted = pair if section + 1 < sections else pair[:1]
            items, *turned = in_vmem(arrive_kernel, wanted, shifted(delta, "item", -section), items)
            items_bf = turned[0] if turned else None
        more = int(section + 1 < sections)
        users, *rounded = users_tail(
            power, bits, runs - 1, words, misfits[-1], chunks[-1], users, u_noise[section], partial, more
        )
        users_bf = rounded[0] if rounded else None
    return (users.reshape(u_factors.shape), items.reshape(v_factors.shape))


def solution(mesh):
    placed = (
        P(("user", "item"), None),
        P(("item", "user"), None),
        P("user", "item", None, None, None, None),
        P("user", "item", None, None),
        P("user", "item", None, None),
        P("user", "item", None),
        P(None, ("user", "item"), None),
        P(None, ("item", "user"), None),
    )
    return jax.shard_map(
        body,
        mesh=mesh,
        in_specs=placed,
        out_specs=(P(("user", "item"), None), P(("item", "user"), None)),
        check_vma=False,
    )
```

```python
import functools
import math

import jax
import jax.numpy as jnp
from jax import lax
from jax.experimental import pallas as pl
from jax.experimental.pallas import tpu as pltpu
from jax.sharding import PartitionSpec as P

HALF_STEP = 0.002
ROOT_STEP = math.sqrt(0.004)
PRIOR = 25.0
GROUP = 4
SCALE_ROWS = 16
SMALL_LIMIT = 12 * 2**20
FETCH_LIMIT = 38 * 2**20
SCALE_STEPS = 128.0
SCALARS = 16
PARTS = 4
LONG = pl.CostEstimate(flops=4 * 10**9, bytes_accessed=2**12, transcendentals=0)
BRIEF = pl.CostEstimate(flops=10**8, bytes_accessed=2**12, transcendentals=0)

ANY = pl.BlockSpec(memory_space=pl.ANY)
IN_HBM = pl.BlockSpec(memory_space=pltpu.HBM)
IN_VMEM = pl.BlockSpec(memory_space=pltpu.VMEM)
IN_SMEM = pl.BlockSpec(memory_space=pltpu.SMEM)


def shifted(x, axis, by):
    peers = lax.axis_size(axis)
    return lax.ppermute(x, axis, [(i, (i + by) % peers) for i in range(peers)])


def swapped(x, axis, mask):
    peers = lax.axis_size(axis)
    return lax.ppermute(x, axis, [(i, i ^ mask) for i in range(peers)])


def routed(x, mask, by):
    across, along = lax.axis_size("user"), lax.axis_size("item")
    pairs = [(u * along + i, (u ^ mask) * along + (i + by) % along) for u in range(across) for i in range(along)]
    return lax.ppermute(x, ("user", "item"), pairs)


def widths(slots, user_tiles, item_tiles):
    bits = tuple(max(1, (n - 1).bit_length()) for n in (slots, user_tiles, item_tiles))
    assert 2 * bits[0] + 2 * bits[1] + bits[2] + 2 <= 31
    return bits


def total(x, axis):
    return jnp.sum(x.astype(jnp.float32), axis=axis, keepdims=True).astype(jnp.int32)


def plan_kernel(section, bits, per, span, runs, me, counts, rows, cols, words, lists):
    slot_bits, row_bits, col_bits = bits
    side = lists.shape[-1]
    slots = rows.shape[-1]
    shape = (side, side)
    count = counts[section]
    lists[...] = jnp.zeros_like(lists)
    lists[0:1, 0:slots] = rows[0, 0, section : section + 1]
    lists[1:2, 0:slots] = cols[0, 0, section : section + 1]
    along = lax.broadcasted_iota(jnp.int32, shape, 1)
    down = lax.broadcasted_iota(jnp.int32, shape, 0)
    row_along = jnp.broadcast_to(lists[0:1], shape)
    place_along = jnp.broadcast_to(lists[1:2] ^ (me[0] * per), shape)
    key = (place_along << row_bits | row_along).astype(jnp.float32).T.astype(jnp.int32)
    row_down = key & ((1 << row_bits) - 1)
    place_down = key >> row_bits
    span_bits = span.bit_length() - 1
    run_along, run_down = place_along >> span_bits, place_down >> span_bits
    live_along, live_down = along < count, down < count
    same = place_along == place_down
    rank_down = total(same & live_along & (row_along < row_down), 1)
    rank_along = total(same & live_down & (row_down < row_along), 0)
    opens = live_along & ((rank_along & 1) == 0)
    within = total(opens & (run_along == run_down) & (place_along < place_down), 1)
    base = jnp.zeros((side, 1), jnp.int32)
    begins = jnp.zeros((1, side), jnp.int32)
    unused = jnp.zeros((1, side), jnp.int32)
    ahead = jnp.zeros((1, 1), jnp.int32)
    for run in range(runs):
        size = total(opens[0:1] & (run_along[0:1] == run), 1)
        size = (size + GROUP - 1) & ~(GROUP - 1)
        base += jnp.where(run_down[:, 0:1] > run, size, 0)
        begins += jnp.where(along[0:1] > side - SCALARS + run, size, 0)
        ahead += size
        unused += jnp.where(along[0:1] >= ahead, span, 0)
    where = base + within + (rank_down >> 1)
    col_at = 2 * slot_bits + 2 * row_bits
    odd = rank_down & 1
    n, row, place = down[:, 0:1], row_down[:, 0:1], place_down[:, 0:1]
    word = jnp.where(odd == 0, n, n << slot_bits)
    word += jnp.where(odd == 0, row, row << row_bits) << (2 * slot_bits)
    word += (jnp.where(odd == 0, place, 0) << col_at) + (1 << (col_at + col_bits))
    word = jnp.broadcast_to(word, shape)
    hit = (where == along) & live_down
    low = total(jnp.where(hit, word & 0xFFFF, 0), 0)
    high = total(jnp.where(hit, word >> 16, 0), 0)
    listed = (high << 16) | low
    unused = jnp.minimum(unused, span * runs - 1) << col_at
    listed = jnp.where(listed == 0, unused, listed)
    words[...] = jnp.where(along[0:1] >= side - SCALARS, begins, listed)


def pair_plan(section, bits, per, span, runs, side, me, counts, rows, cols):
    return pl.pallas_call(
        functools.partial(plan_kernel, section, bits, per, span, runs),
        out_shape=jax.ShapeDtypeStruct((1, side), jnp.int32),
        in_specs=[IN_SMEM, IN_SMEM, IN_VMEM, IN_VMEM],
        out_specs=IN_VMEM,
        scratch_shapes=[pltpu.VMEM((8, side), jnp.int32)],
        compiler_params=pltpu.CompilerParams(vmem_limit_bytes=SMALL_LIMIT),
        cost_estimate=LONG,
    )(me, counts, rows, cols)


def bounds(words, run):
    at = words.shape[-1] - SCALARS + run
    return words[0, at], words[0, at + 1]


def decode_word(word, bits, first_col):
    slot_bits, row_bits, col_bits = bits
    fields = []
    for width in (slot_bits, slot_bits, row_bits, row_bits, col_bits):
        fields.append(word & ((1 << width) - 1))
        word = word >> width
    fields[4] -= first_col
    return (*fields, word)


def fetch_kernel(lump, counts, ratings, out, sem):
    def loads(section):
        def load(i):
            part = pl.ds(i * lump, lump)
            return pltpu.make_async_copy(ratings.at[section, part], out.at[section, part], sem.at[section, i])

        return lax.div(counts[section] + lump - 1, lump), load

    for section in range(ratings.shape[0]):
        lumps, load = loads(section)
        lax.fori_loop(0, lumps, lambda i, c, load=load: (load(i).start(), c)[1], 0)
    for section in range(ratings.shape[0]):
        lumps, load = loads(section)
        lax.fori_loop(0, lumps, lambda i, c, load=load: (load(i).wait(), c)[1], 0)


def fetch(counts, ratings):
    sections, slots = ratings.shape[:2]
    lump = math.gcd(slots, 16)
    return pl.pallas_call(
        functools.partial(fetch_kernel, lump),
        out_shape=jax.ShapeDtypeStruct(ratings.shape, ratings.dtype),
        in_specs=[IN_SMEM, IN_HBM],
        out_specs=IN_VMEM,
        scratch_shapes=[pltpu.SemaphoreType.DMA((sections, slots // lump))],
        compiler_params=pltpu.CompilerParams(vmem_limit_bytes=FETCH_LIMIT),
        cost_estimate=LONG,
    )(counts, ratings)


def gather_tiles(pieces, items):
    at = 0
    for piece in pieces:
        for t in range(piece.shape[0]):
            items[at + t] = piece[t]
        at += piece.shape[0]


def items_kernel(section, run, count, skipped, bits, listed, ratings, users, *refs):
    outs = refs[count + skipped : -4]
    items, grad, words, sem = refs[-4:]
    load = pltpu.make_async_copy(listed, words, sem)
    load.start()
    out_even, *out_odd, misfits = outs
    span = items.shape[0]
    per = span // 2
    tile = users.shape[1]
    gather_tiles(refs[:count], items)
    grad[...] = jnp.zeros_like(grad)
    load.wait()
    low, high = bounds(words, run)
    steps = lax.div(high - low, GROUP)

    def decode(p):
        return decode_word(words[0, p], bits, run * span)

    def users_of(row_a, row_b):
        return jnp.concatenate([users[row_a], users[row_b]], axis=0)

    def predict(p):
        slot_a, slot_b, row_a, row_b, col, live = decode(p)
        predicted = lax.dot_general(
            users_of(row_a, row_b), items[col], (((1,), (0,)), ((), ())), preferred_element_type=jnp.float32
        )
        given = jnp.concatenate([ratings[section, slot_a], ratings[section, slot_b]], axis=0).astype(jnp.float32)
        rows = lax.broadcasted_iota(jnp.int32, (2 * tile, 1), 0)
        return jnp.where(rows < tile * live, given - predicted, 0.0).astype(jnp.bfloat16)

    def add_grad(p, misfit):
        _, _, row_a, row_b, col, _ = decode(p)
        grad[col] += lax.dot_general(
            misfit, users_of(row_a, row_b), (((0,), (0,)), ((), ())), preferred_element_type=jnp.float32
        )

    @pl.when(steps > 0)
    def _():
        for j in range(GROUP):
            misfits[j] = predict(low + j)

        def advance(step, carry):
            at = step * GROUP
            held = [misfits[at + j] for j in range(GROUP)]
            following = [predict(low + at + GROUP + j) for j in range(GROUP)]
            for j in range(GROUP):
                add_grad(low + at + j, held[j])
            for j in range(GROUP):
                misfits[at + GROUP + j] = following[j]
            return carry

        lax.fori_loop(0, steps - 1, advance, 0)
        for j in range(GROUP):
            add_grad(high - GROUP + j, misfits[high - low - GROUP + j])

    at = 0
    for out in (out_even, *out_odd):
        for t in range(out.shape[0]):
            out[t] = grad[at + t]
        at += out.shape[0]


def item_grads(section, run, per, bits, words, ratings, users, pieces, after, parts):
    tile, width = users.shape[1:]
    f32 = jnp.float32
    held = per * (users.shape[0] + users.shape[0] % 2)
    held = -(-min(held, ratings.shape[1] // 2 + per) // GROUP) * GROUP
    even_grad, *odd_grads, misfits = pl.pallas_call(
        functools.partial(items_kernel, section, run, len(pieces), len(after), bits),
        out_shape=[jax.ShapeDtypeStruct((per, tile, width), f32)]
        + [jax.ShapeDtypeStruct((per // parts, tile, width), f32)] * parts
        + [jax.ShapeDtypeStruct((held, 2 * tile, tile), jnp.bfloat16)],
        in_specs=[ANY] + [IN_VMEM] * (2 + len(pieces)) + [ANY] * len(after),
        out_specs=[IN_VMEM] * (2 + parts),
        scratch_shapes=[
            pltpu.VMEM((2 * per, width, tile), jnp.bfloat16),
            pltpu.VMEM((2 * per, tile, width), f32),
            pltpu.SMEM(words.shape, jnp.int32),
            pltpu.SemaphoreType.DMA,
        ],
        compiler_params=pltpu.CompilerParams(vmem_limit_bytes=SMALL_LIMIT),
        cost_estimate=LONG,
    )(words, ratings, users, *pieces, *after)
    return even_grad, odd_grads, misfits


def add_user_grads(bits, first_run, words, pieces, misfits, items, grad):
    tile = grad.shape[1]
    first_col = first_run * items.shape[0] // len(misfits)
    gather_tiles(pieces, items)
    for run, held in enumerate(misfits, first_run):
        low, high = bounds(words, run)

        def advance(step, carry, low=low, held=held):
            for j in range(GROUP):
                at = step * GROUP + j
                _, _, row_a, row_b, col, _ = decode_word(words[0, low + at], bits, first_col)
                part = lax.dot_general(
                    held[at], items[col], (((1,), (1,)), ((), ())), preferred_element_type=jnp.float32
                )
                grad[row_a] += part[:tile]
                grad[row_b] += part[tile:]
            return carry

        lax.fori_loop(0, lax.div(high - low, GROUP), advance, 0)


def users_head_kernel(bits, runs, words, *refs):
    *pieces, _, grad, items = refs[runs:]
    grad[...] = jnp.zeros_like(grad)
    add_user_grads(bits, 0, words, pieces, refs[:runs], items, grad)


def users_tail_kernel(power, bits, first_run, words, held, *refs):
    *pieces, factors, noise, partial, new, new_bf, items, grad = refs
    grad[...] = partial[...]
    add_user_grads(bits, first_run, words, pieces, [held], items, grad)

    def finish(t, carry):
        before = factors[t]
        after = (
            before + HALF_STEP * (power * grad[t] - PRIOR * before) + ROOT_STEP * noise[t].astype(jnp.float32)
        )
        new[t] = after
        new_bf[t] = after.astype(jnp.bfloat16)
        return carry

    lax.fori_loop(0, factors.shape[0], finish, 0)


def tiles_of(pieces):
    return sum(piece.shape[0] for piece in pieces), *pieces[0].shape[1:]


def users_head(bits, words, misfits, pieces, shape, after):
    return pl.pallas_call(
        functools.partial(users_head_kernel, bits, len(misfits)),
        out_shape=jax.ShapeDtypeStruct(shape, jnp.float32),
        in_specs=[IN_SMEM] + [IN_VMEM] * (len(misfits) + len(pieces)) + [ANY],
        out_specs=IN_VMEM,
        scratch_shapes=[pltpu.VMEM(tiles_of(pieces), jnp.bfloat16)],
        compiler_params=pltpu.CompilerParams(vmem_limit_bytes=SMALL_LIMIT),
        cost_estimate=BRIEF,
    )(words, *misfits, *pieces, after)


def users_tail(power, bits, first_run, words, misfits, pieces, factors, noise, partial):
    shape = factors.shape
    return pl.pallas_call(
        functools.partial(users_tail_kernel, power, bits, first_run),
        out_shape=[jax.ShapeDtypeStruct(shape, jnp.float32), jax.ShapeDtypeStruct(shape, jnp.bfloat16)],
        in_specs=[IN_SMEM, IN_VMEM] + [IN_VMEM] * (len(pieces) + 3),
        out_specs=[IN_VMEM] * 2,
        scratch_shapes=[pltpu.VMEM(tiles_of(pieces), jnp.bfloat16), pltpu.VMEM(shape, jnp.float32)],
        compiler_params=pltpu.CompilerParams(vmem_limit_bytes=SMALL_LIMIT),
        cost_estimate=BRIEF,
    )(words, misfits, *pieces, factors, noise, partial)


def coded_shape(per, tile, width):
    return jax.ShapeDtypeStruct((per * tile + SCALE_ROWS, width), jnp.int16)


def encode(blocks, out):
    per = len(blocks)
    tile, width = blocks[0].shape
    row = lax.broadcasted_iota(jnp.int32, (SCALE_ROWS, width), 0)
    powers = jnp.zeros((SCALE_ROWS, width), jnp.int32)
    for t, block in enumerate(blocks):
        largest = jnp.max(jnp.abs(block), axis=0, keepdims=True)
        power = jnp.ceil(SCALE_STEPS * jnp.log2(jnp.maximum(largest, 1e-20)))
        scaled = jnp.round(block * jnp.exp2(15.0 - power / SCALE_STEPS))
        out[pl.ds(t * tile, tile)] = jnp.clip(scaled, -32767.0, 32767.0).astype(jnp.int32).astype(jnp.int16)
        powers = jnp.where(row == t, power.astype(jnp.int32), powers)
    out[pl.ds(per * tile, SCALE_ROWS)] = powers.astype(jnp.int16)


def decoded(ref, t, tile, per):
    powers = ref[pl.ds(per * tile, SCALE_ROWS)].astype(jnp.int32).astype(jnp.float32)
    unit = jnp.exp2(powers[t : t + 1] / SCALE_STEPS - 15.0)
    return ref[pl.ds(t * tile, tile)].astype(jnp.int32).astype(jnp.float32) * unit


def join_kernel(count, mine, *refs):
    others = [ref[t] for ref in refs[:count] for t in range(ref.shape[0])]
    encode([mine[t] + other for t, other in enumerate(others)], refs[-1])


def join(mine, others, after):
    return pl.pallas_call(
        functools.partial(join_kernel, len(others)),
        out_shape=coded_shape(*mine.shape),
        in_specs=[IN_VMEM] * (1 + len(others)) + [ANY] * len(after),
        out_specs=IN_VMEM,
        compiler_params=pltpu.CompilerParams(vmem_limit_bytes=SMALL_LIMIT),
        cost_estimate=BRIEF,
    )(mine, *others, *after)


def owner_sum(mine, other, coded, t):
    per, tile, _ = mine.shape
    total = mine[t] + other[t]
    for ref in coded:
        total = total + decoded(ref, t, tile, per)
    return total


def update_kernel(power, mine, other, *refs):
    *coded, factors, noise, _, new, new_bf = refs
    for t in range(mine.shape[0]):
        step = HALF_STEP * power * owner_sum(mine, other, coded, t) + ROOT_STEP * noise[t].astype(jnp.float32)
        after = factors[t] - HALF_STEP * PRIOR * factors[t] + step
        new[t] = after
        new_bf[t] = after.astype(jnp.bfloat16).T


def delta_kernel(power, parts, count, mine, noise, *refs):
    per, tile, _ = mine.shape
    others = [ref[t] for ref in refs[:parts] for t in range(ref.shape[0])]
    steps = []
    for t in range(per):
        grad = mine[t] + others[t]
        for coded in refs[parts : parts + count]:
            grad = grad + decoded(coded, t, tile, per)
        steps.append(HALF_STEP * power * grad + ROOT_STEP * noise[t].astype(jnp.float32))
    encode(steps, refs[-1])


def arrive_kernel(power, count, factors, delta, *refs):
    per, tile, _ = factors.shape
    for t in range(per):
        grad = sum(decoded(ref, t, tile, per) for ref in refs[:count])
        after = factors[t] - HALF_STEP * PRIOR * factors[t] + decoded(delta, t, tile, per)
        after = after + HALF_STEP * power * grad
        refs[count][t] = after
        for out in refs[count + 1 :]:
            out[t] = after.astype(jnp.bfloat16).T


def turn_kernel(factors, out):
    for t in range(factors.shape[0]):
        out[t] = factors[t].astype(jnp.bfloat16).T


def pass_kernel(given, *refs):
    refs[-1][...] = given[...]


def in_vmem(kernel, out_shape, *operands, after=()):
    return pl.pallas_call(
        kernel,
        out_shape=out_shape,
        in_specs=[IN_VMEM] * len(operands) + [ANY] * len(after),
        out_specs=jax.tree.map(lambda _: IN_VMEM, out_shape),
        compiler_params=pltpu.CompilerParams(vmem_limit_bytes=SMALL_LIMIT),
        cost_estimate=BRIEF,
    )(*operands, *after)


def gathered(own, runs):
    evens = [own]
    for d in range(1, runs):
        relayed = runs == 4 and d == 3
        evens.append(swapped(evens[1] if relayed else own, "user", 4 if relayed else 2 * d))
    return evens


def body(u_factors, v_factors, ratings, tile_rows, tile_cols, tile_counts, u_noise, v_noise):
    tile = ratings.shape[-1]
    sections = ratings.shape[2]
    width = u_factors.shape[1]
    peers = lax.axis_size("user")
    power = float(lax.axis_size("item"))
    me = lax.axis_index("user").astype(jnp.int32).reshape(1)
    users = u_factors.reshape(-1, tile, width)
    items = v_factors.reshape(-1, tile, width)
    per = items.shape[0]
    item_tiles = peers * per
    span = 2 * per
    runs = item_tiles // span
    ratings = ratings.reshape(ratings.shape[2:])
    counts = tile_counts.reshape(sections)
    u_noise = u_noise.reshape(sections, *users.shape)
    v_noise = v_noise.reshape(sections, *items.shape)
    side = -(-ratings.shape[1] // 128) * 128
    assert (ratings.shape[1] + item_tiles) // 2 + runs * GROUP <= side - SCALARS and runs < SCALARS
    assert per & (per - 1) == 0
    bits = widths(ratings.shape[1], users.shape[0], item_tiles)
    pair = (
        jax.ShapeDtypeStruct(items.shape, jnp.float32),
        jax.ShapeDtypeStruct((per, width, tile), jnp.bfloat16),
    )
    rated = fetch(counts, ratings)
    items_bf = in_vmem(turn_kernel, pair[1], items)
    users_bf = users.astype(jnp.bfloat16)
    for section in range(sections):
        words = pair_plan(section, bits, per, span, runs, side, me, counts, tile_rows, tile_cols)
        sent = items_bf
        if section:
            sent = shifted(items_bf, "item", section)
            sent = in_vmem(pass_kernel, jax.ShapeDtypeStruct(sent.shape, sent.dtype), sent, after=(users_bf, words))
        evens = gathered(sent, runs)
        chunks = [[even, swapped(even, "user", 1)] for even in evens]
        mine, other, sums, misfits = {}, {}, {}, {}
        after = [evens[2]]
        order = [(item_grads, run) for run in range(1, runs - 1)]
        order += [(join, run) for run in range(1, runs - 1)]
        order += [(item_grads, runs - 1), (item_grads, 0), (join, runs - 1)]
        for call, run in order:
            if call is item_grads:
                parts = 1 if not run else 2
                if section and not run:
                    parts = min(PARTS, per)
                mine[run], odd_grads, misfits[run] = item_grads(
                    section, run, per, bits, words, rated, users_bf, chunks[run], after, parts
                )
                other[run] = [swapped(grad, "user", 1) for grad in odd_grads]
                after = [mine[run]]
            else:
                if run == runs - 1 and not section:
                    after += list(sums.values())
                after = [join(mine[run], other[run], after)]
                if section and run == runs - 1:
                    sums[run] = routed(after[0], 2 * run, -section)
                else:
                    sums[run] = swapped(after[0], "user", 2 * run)
        if section:
            near = [sums[run] for run in range(1, runs - 1)]
            share = functools.partial(delta_kernel, power, len(other[0]), len(near))
            share = in_vmem(
                share, coded_shape(*items.shape), mine[0], v_noise[section], *other[0], *near, after=after
            )
        sums = [sums[run] for run in range(1, runs)]
        misfits = [misfits[run] for run in range(runs)]
        head = [piece for chunk in chunks[:-1] for piece in chunk]
        partial = users_head(bits, words, misfits[:-1], head, users.shape, after[0])
        if section == 0:
            items, items_bf = in_vmem(
                functools.partial(update_kernel, power),
                pair,
                mine[0],
                other[0][0],
                *sums,
                items,
                v_noise[section],
                after=(partial,),
            )
        else:
            wanted = pair if section + 1 < sections else pair[:1]
            arrive = functools.partial(arrive_kernel, power, 1)
            items, *turned = in_vmem(arrive, wanted, items, routed(share, 0, -section), sums[-1])
            items_bf = turned[0] if turned else None
        users, users_bf = users_tail(
            power, bits, runs - 1, words, misfits[-1], chunks[-1], users, u_noise[section], partial
        )
    return (users.reshape(u_factors.shape), items.reshape(v_factors.shape))


def solution(mesh):
    placed = (
        P(("user", "item"), None),
        P(("item", "user"), None),
        P("user", "item", None, None, None, None),
        P("user", "item", None, None),
        P("user", "item", None, None),
        P("user", "item", None),
        P(None, ("user", "item"), None),
        P(None, ("item", "user"), None),
    )
    return jax.shard_map(
        body,
        mesh=mesh,
        in_specs=placed,
        out_specs=(P(("user", "item"), None), P(("item", "user"), None)),
        check_vma=False,
    )
```
